128 devices in a mesh: blk: 16 (over x_lo, y, core), node: 8 (over x_hi, z).
Axes of the slice: x: 4 (x_hi: 2, x_lo: 2; x = x_hi * 2 + x_lo), y: 4, z: 4, core: 2. Of those that a mesh axis runs over, the one named last changes fastest.
Arguments:
- images: bfloat16 [49152, 1280], P(('blk', 'node')), may hold values from -11 to 11
- texts: bfloat16 [49152, 1280], P(('blk', 'node')), may hold values from -0.4 to 0.4
- rest_row: float32 [49152], P(('blk', 'node')), may hold values from 2 to 20
- rest_col: float32 [49152], P(('blk', 'node')), may hold values from 2 to 20
Outputs:
- image_grad: float32 [49152, 1280], P(('blk', 'node'))
- text_grad: float32 [49152, 1280], P(('blk', 'node'))
- loss: float32 [], replicated
The draws below stay inside these ranges and needn't reach their ends.
All inputs are finite; a program needn't handle non-finite values.
Results may differ from the reference program's by a relative error of at most 0.00105.
The reference program's roundings to bfloat16 on the way count: a program that leaves them out, or rounds other values in their place, can miss the bound.
Values may be sent and summed in bfloat16 or wider, within the bound.
A program may use at most 192 MiB of HBM per device.

```python
import math
import jax
import jax.numpy as jnp
from jax import lax

EMBED = 1280
ROWS = 384
GROUP = 3072
TOKENS = 49152
N_BLK = 16
N_NODE = 8


def shared_texts(key):
    spread = 0.173 * EMBED ** (-0.25)
    normal_part = jnp.clip(jax.random.normal(jax.random.fold_in(key, 101), (TOKENS, EMBED), jnp.float32), -6.0, 6.0)
    return normal_part * spread


def draw_texts(key, part):
    normal_texts = shared_texts(key)
    values = normal_texts
    return values.astype(jnp.bfloat16)


def paired_rows(key, base, own, top_strength):
    factor = 36.7 / math.sqrt(EMBED)
    strength = jax.random.uniform(jax.random.fold_in(key, 2), (TOKENS, 1), jnp.float32, 1.0, top_strength)
    aligned = strength * factor * (own + 0.97 * jnp.roll(own, -1, axis=0))
    picked = (jnp.arange(TOKENS, dtype=jnp.int32) % 64 == 5)[:, None]
    return jnp.where(picked, aligned, base)


def draw_images(key, part):
    normal_texts = shared_texts(key)
    key = jax.random.fold_in(key, 7)
    spread = 0.173 * EMBED ** (-0.25)
    base = jnp.clip(jax.random.normal(jax.random.fold_in(key, 1), (TOKENS, EMBED), jnp.float32), -6.0, 6.0) * spread
    values = paired_rows(key, base, normal_texts, 1.3)
    return values.astype(jnp.bfloat16)


def draw_rest_row(key, part):
    key = jax.random.fold_in(key, 11)
    return math.log(2.0 * GROUP) + jax.random.uniform(key, (TOKENS,), jnp.float32, 2.0, 7.0)


def draw_rest_col(key, part):
    key = jax.random.fold_in(key, 13)
    return math.log(2.0 * GROUP) + jax.random.uniform(key, (TOKENS,), jnp.float32, 2.0, 7.0)


def setup_inputs(seed: int = 0) -> dict:
    seeds = jax.random.split(jax.random.key(seed), 5)
    images = draw_images(jax.random.fold_in(seeds[4], 71), 0)
    texts = draw_texts(jax.random.fold_in(seeds[4], 71), 0)
    rest_row = draw_rest_row(jax.random.fold_in(seeds[4], 71), 0)
    rest_col = draw_rest_col(jax.random.fold_in(seeds[4], 71), 0)
    return dict(images=images, texts=texts, rest_row=rest_row, rest_col=rest_col)


logit_scale = 100.0


def merge_pair(first, second):
    top = jnp.maximum(first[0], second[0])
    return top, first[1] * jnp.exp(first[0] - top) + second[1] * jnp.exp(second[0] - top)


def reference(images, texts, rest_row, rest_col):
    group = N_NODE * ROWS
    image_groups = images.reshape(N_BLK, group, EMBED)
    text_groups = texts.reshape(N_BLK, group, EMBED)
    prev_texts = jnp.roll(text_groups, 1, axis=0)
    order = jnp.arange(N_BLK, dtype=jnp.int32)

    def block_logits(index):
        window = jnp.concatenate([prev_texts[index], text_groups[index]], 0)
        logits = logit_scale * lax.dot_general(image_groups[index], window, (((1,), (1,)), ((), ())), preferred_element_type=jnp.float32)
        return logits, window

    def stats(index):
        logits, window = block_logits(index)
        row_part = jax.nn.logsumexp(logits, axis=1)
        col_max = jnp.max(logits, axis=0)
        col_sum = jnp.sum(jnp.exp(logits - col_max[None, :]), axis=0)
        diag = jnp.diagonal(logits[:, group:])
        return row_part, col_max, col_sum, diag

    row_part, col_max, col_sum, diag = lax.map(stats, order)
    row_lse = jnp.logaddexp(rest_row.reshape(N_BLK, group), row_part)
    own_max, own_sum = merge_pair((col_max[:, group:], col_sum[:, group:]), (jnp.roll(col_max[:, :group], -1, axis=0), jnp.roll(col_sum[:, :group], -1, axis=0)))
    col_lse = jnp.logaddexp(rest_col.reshape(N_BLK, group), own_max + jnp.log(own_sum))
    prev_col = jnp.roll(col_lse, 1, axis=0)
    loss = (jnp.sum(row_lse) + jnp.sum(col_lse) - 2.0 * jnp.sum(diag)) / (2.0 * TOKENS)

    def grads(index):
        logits, window = block_logits(index)
        col_window = jnp.concatenate([prev_col[index], col_lse[index]], 0)
        marks = jnp.concatenate([jnp.zeros((group, group), jnp.float32), jnp.eye(group, dtype=jnp.float32)], 1)
        weights = jnp.exp(logits - row_lse[index][:, None]) + jnp.exp(logits - col_window[None, :]) - 2.0 * marks
        weights = weights.astype(jnp.bfloat16)
        image_part = logit_scale * jnp.dot(weights, window, preferred_element_type=jnp.float32)
        text_part = logit_scale * lax.dot_general(weights, image_groups[index], (((0,), (0,)), ((), ())), preferred_element_type=jnp.float32)
        return image_part, text_part

    image_part, text_part = lax.map(grads, order)
    image_grad = image_part.reshape(TOKENS, EMBED)
    text_grad = (text_part[:, group:] + jnp.roll(text_part[:, :group], -1, axis=0)).reshape(TOKENS, EMBED)
    return image_grad, text_grad, loss
```

```python
import functools

import jax
import jax.numpy as jnp
from jax import lax
from jax.experimental import pallas as pl
from jax.experimental.pallas import tpu as pltpu
from jax.sharding import PartitionSpec as P


MESH = pl.DeviceIdType.MESH
F32, BF16 = jnp.float32, jnp.bfloat16
logit_scale = 100.0
LANES = 128
CHUNK = 16
PAD = 16
WIDE = 256
POWER_RANGE = 2.0**18

(IMG_R0, IMG_R1, IMG_L1, IMG_L0, FWD_R, FWD_L, TXT_X0, TXT_X1, TXT_N0, TXT_N1, FWD_N0, FWD_N1) = range(12)
(ROW_R, ROW_L, ROW_F, OWN_X, OWN_NS, OWN_NO, PRV_X, PRV_PS, PRV_PO) = range(12, 21)
OUT = 21
(F_R, F_L, R_DIR, L_DIR, R_ACC, L_ACC, Y_0, Y_1, Y_2, Y_3, X_0, X_1) = range(12)
UNITS = 12
SUM = OUT + UNITS


def kernel(
    n_blk, img_ref, txt_ref, rr_ref, rc_ref, ig_ref, tg_ref, loss_ref,
    im, tx, s_ref, w, wt, rowp, colm, cols, rstat, rl, co, cp, cl, keep, snd, rcv, lsnd, lrcv,
    ss, rs, lsem,
):
    rows, width = img_ref.shape
    half = rows // 2
    tile = 4 * rows
    b = lax.axis_index("blk")
    node = lax.axis_index("node")
    i, z = node // 4, node % 4
    zr, zl, zf = (z + 1) % 4, (z + 3) % 4, (z + 2) % 4
    nxt, prv = (b + 1) % n_blk, (b + n_blk - 1) % n_blk
    oi = 1 - i

    def dev(blk, hi, zz):
        return (blk, hi * 4 + zz)

    right, left, far = dev(b, i, zr), dev(b, i, zl), dev(b, i, zf)
    across = dev(b, oi, z)
    n_same, n_other, p_same, p_other = dev(nxt, i, z), dev(nxt, oi, z), dev(prv, i, z), dev(prv, oi, z)

    def flip(value, step):
        return value + step - 2 * step * ((value // step) % 2)

    steps, step = [], 1
    while step < n_blk:
        steps.append(step)
        step *= 2
    flips = [dev(b, i, flip(z, 1)), far, across] + [dev(flip(b, step), i, z) for step in steps]

    load_img = pltpu.make_async_copy(img_ref, im.at[pl.ds(pl.multiple_of(z * rows, rows), rows)], lsem.at[0])
    load_txt = pltpu.make_async_copy(txt_ref, tx.at[pl.ds(pl.multiple_of(i * rows, rows), rows)], lsem.at[1])
    load_img.start()
    load_txt.start()

    barrier = pltpu.get_barrier_semaphore()
    partners = [right, left, far, across, n_same, n_other, p_same, p_other]
    partners += [dev(flip(b, step), i, z) for step in steps[1:]]
    for partner in partners:
        pl.semaphore_signal(barrier, inc=1, device_id=partner, device_id_type=MESH)
    pl.semaphore_wait(barrier, len(partners))
    load_img.wait()
    load_txt.wait()

    def remote(k, src, dst, target):
        return pltpu.make_async_remote_copy(
            src_ref=src, dst_ref=dst, send_sem=ss.at[k], recv_sem=rs.at[k], device_id=target, device_id_type=MESH
        )

    def block(slot):
        return pl.ds(pl.multiple_of(slot * rows, rows), rows)

    def part(slot, h):
        return pl.ds(pl.multiple_of(slot * rows + h * half, half), half)

    copies = {}

    def send(k, src, dst, target):
        copies[k] = remote(k, src, dst, target)
        copies[k].start()

    def same(k, ref, where, target):
        send(k, ref.at[where], ref.at[where], target)

    same(IMG_R0, im, part(z, 0), right)
    same(IMG_L1, im, part(z, 1), left)
    same(TXT_X0, tx, part(i, 0), across)
    send(TXT_N0, tx.at[part(i, 0)], tx.at[part(2 + i, 0)], n_same)
    same(IMG_R1, im, part(z, 1), right)
    same(IMG_L0, im, part(z, 0), left)
    same(TXT_X1, tx, part(i, 1), across)
    send(TXT_N1, tx.at[part(i, 1)], tx.at[part(2 + i, 1)], n_same)
    copies[IMG_R0].wait_recv()
    same(FWD_R, im, part(zl, 0), right)
    copies[IMG_L1].wait_recv()
    same(FWD_L, im, part(zr, 1), left)
    copies[TXT_X0].wait_recv()
    send(FWD_N0, tx.at[part(oi, 0)], tx.at[part(2 + oi, 0)], n_same)
    copies[TXT_X1].wait_recv()
    send(FWD_N1, tx.at[part(oi, 1)], tx.at[part(2 + oi, 1)], n_same)
    for k in (TXT_N0, TXT_N1, FWD_N0, FWD_N1):
        copies[k].wait_recv()

    n_chunks = rows // CHUNK
    n_lane = tile // LANES
    lanes = lambda k: pl.ds(k * LANES, LANES)

    def logits_block(q, order):
        base = pl.multiple_of(q * rows, rows)

        @pl.loop(0, 4)
        def _(c):
            span = pl.ds(pl.multiple_of(c * rows, rows), rows)
            s_ref[block(q), span] = logit_scale * lax.dot_general(
                im[block(q), :], tx[span, :], (((1,), (1,)), ((), ())), preferred_element_type=F32
            )

        def chunk(r):
            return pl.ds(pl.multiple_of(base + r * CHUNK, CHUNK), CHUNK)

        def row_pass(r, top):
            s = s_ref[chunk(r), :]
            m = jnp.max(s, axis=1, keepdims=True)
            total = jnp.sum(jnp.exp(s - m), axis=1, keepdims=True)
            rowp[chunk(r), :] = jnp.broadcast_to(m + jnp.log(total), (CHUNK, LANES))
            return jnp.maximum(top, jnp.maximum(s[:8], s[8:]))

        top = lax.fori_loop(0, n_chunks, row_pass, jnp.full((8, tile), -jnp.inf, F32))
        top = jnp.broadcast_to(jnp.max(top, axis=0, keepdims=True), (8, tile))

        def col_pass(r, total):
            s = s_ref[chunk(r), :]
            return total + jnp.exp(s[:8] - top) + jnp.exp(s[8:] - top)

        total = lax.fori_loop(0, n_chunks, col_pass, jnp.zeros((8, tile), F32))
        colm[pl.ds(order * 8, 8), :] = top
        cols[pl.ds(order * 8, 8), :] = jnp.broadcast_to(jnp.sum(total, axis=0, keepdims=True), (8, tile))
        rstat[:, block(q)] = jnp.transpose(rowp[block(q), :])[:8, :]

    logits_block(z, 0)
    copies[IMG_R1].wait_recv()
    logits_block(zl, 1)
    copies[IMG_L0].wait_recv()
    logits_block(zr, 2)
    copies[FWD_R].wait_recv()
    copies[FWD_L].wait_recv()
    logits_block(zf, 3)

    def join(a, c):
        top = jnp.maximum(a, c)
        return top + jnp.log(jnp.exp(a - top) + jnp.exp(c - top))

    rstat[:, block(z)] = join(rstat[:, block(z)], jnp.broadcast_to(rr_ref[...], (8, rows)))
    rl[z] = rstat[...]
    for k, target in ((ROW_R, right), (ROW_L, left), (ROW_F, far)):
        send(k, rstat, rl.at[z], target)
    top = functools.reduce(jnp.maximum, [colm[pl.ds(8 * k, 8), :] for k in range(4)])
    total = functools.reduce(
        jnp.add, [cols[pl.ds(8 * k, 8), :] * jnp.exp(colm[pl.ds(8 * k, 8), :] - top) for k in range(4)]
    )
    both = top + jnp.log(total)
    co[i] = both[:, : 2 * rows]
    cp[2 + i] = both[:, 2 * rows :]
    co[i, :, block(i)] = join(co[i, :, block(i)], jnp.broadcast_to(rc_ref[...], (8, rows)))
    send(OWN_X, co.at[i], co.at[i], across)
    send(OWN_NS, co.at[i], cp.at[i], n_same)
    send(OWN_NO, co.at[i], cp.at[i], n_other)
    send(PRV_X, cp.at[2 + i], cp.at[2 + i], across)
    send(PRV_PS, cp.at[2 + i], co.at[2 + i], p_same)
    send(PRV_PO, cp.at[2 + i], co.at[2 + i], p_other)

    def diag_pass(r, total):
        s = s_ref[pl.ds(pl.multiple_of(z * rows + r * CHUNK, CHUNK), CHUNK), block(i)]
        row = lax.broadcasted_iota(jnp.int32, s.shape, 0) + r * CHUNK
        return total + jnp.where(lax.broadcasted_iota(jnp.int32, s.shape, 1) == row, s, 0.0)

    diag = jnp.sum(lax.fori_loop(0, n_chunks, diag_pass, jnp.zeros((CHUNK, rows), F32)), keepdims=True)

    def merged(parts):
        top = functools.reduce(jnp.maximum, parts)
        return top + jnp.log(functools.reduce(jnp.add, [jnp.exp(p - top) for p in parts]))

    for k in range(ROW_R, PRV_PO + 1):
        copies[k].wait_recv()
    cl[:, : 2 * rows] = merged([co[k] for k in range(4)])
    cl[:, 2 * rows :] = merged([cp[k] for k in range(4)])
    rstat2 = merged([rl[k] for k in range(4)])
    for q in range(4):
        column = jnp.broadcast_to(rstat2[0:1, q * rows : (q + 1) * rows], (LANES, rows))
        rowp[pl.ds(q * rows, rows), :] = jnp.transpose(column)

    terms = (
        jnp.sum(rowp[block(z), 0:1], keepdims=True)
        + jnp.sum(cl[0:1, block(i)], keepdims=True)
        - 2.0 * diag
    )
    loss_ref[...] = jnp.broadcast_to(terms, loss_ref.shape)

    def loss_send(k):
        lsnd[k] = loss_ref[...]
        send(SUM + k, lsnd.at[k], lrcv.at[k], flips[k])

    def loss_next(k):
        copies[SUM + k].wait_recv()
        loss_ref[...] = lsnd[k] + lrcv[k]

    def weights_block(q):
        mine = q == z

        @pl.loop(0, n_chunks)
        def _(r):
            where = pl.ds(pl.multiple_of(q * rows + r * CHUNK, CHUNK), CHUNK)
            row_lse = rowp[where, :]
            row = lax.broadcasted_iota(jnp.int32, (CHUNK, LANES), 0) + (r * CHUNK + i * rows)
            target = jnp.where(mine, row, -1) - lax.broadcasted_iota(jnp.int32, (CHUNK, LANES), 1)
            for k in range(n_lane):
                s = s_ref[where, lanes(k)]
                value = jnp.exp(s - row_lse) + jnp.exp(s - cl[0:1, lanes(k)])
                if k < n_lane // 2:
                    value = value - jnp.where(target == k * LANES, 2.0, 0.0)
                w[where, lanes(k)] = value.astype(BF16)

    def turn_block(q):
        @pl.loop(0, 4)
        def _(t):
            wt[block(t), block(q)] = jnp.transpose(w[block(q), block(t)])

    def product(left_ref, slot, right_ref, span):
        return logit_scale * jnp.dot(left_ref[block(slot), :], right_ref[:, span], preferred_element_type=F32)

    def encode(value, unit, span):
        top = jnp.maximum(jnp.max(jnp.abs(value), axis=0, keepdims=True), 1e-30)
        snd[unit, pl.ds(half, PAD), span] = jnp.broadcast_to(top, (PAD, WIDE)).astype(BF16)
        top = snd[unit, pl.ds(half, PAD), span].astype(F32)[0:1]
        u = value * (POWER_RANGE / top)
        u2 = u * u
        u4 = u2 * u2
        snd[unit, pl.ds(0, half), span] = (u4 * u2 * u).astype(BF16)

    def decode(unit, span):
        code = rcv[unit, pl.ds(0, half), span].astype(F32)
        top = rcv[unit, pl.ds(half, PAD), span].astype(F32)[0:1] * (1.0 / POWER_RANGE)
        size = jnp.abs(code)
        root = jnp.exp2(jnp.log2(size) * (1.0 / 7.0))
        return jnp.where(size > 0.0, jnp.where(code < 0.0, -root, root), 0.0) * top

    def unit_send(unit, target):
        send(OUT + unit, snd.at[unit], rcv.at[unit], target)

    def arrived(unit):
        copies[OUT + unit].wait_recv()

    def columns(body):
        @pl.loop(0, width // WIDE)
        def _(n):
            body(pl.ds(pl.multiple_of(n * WIDE, WIDE), WIDE))

    lo, hi = pl.ds(0, half), pl.ds(half, half)

    weights_block(zf)

    @columns
    def _(span):
        value = product(w, zf, tx, span)
        encode(value[:half], F_R, span)
        encode(value[half:], F_L, span)

    unit_send(F_R, right)
    unit_send(F_L, left)
    loss_send(0)

    weights_block(zr)
    weights_block(zl)
    weights_block(z)
    for q in range(4):
        turn_block(q)

    @columns
    def _(span):
        value = product(wt, 2 + oi, im, span)
        encode(value[:half], Y_0, span)
        encode(value[half:], Y_1, span)

    unit_send(Y_0, p_same)
    unit_send(Y_1, p_same)
    loss_next(0)
    loss_send(1)

    @columns
    def _(span):
        value = product(w, zr, tx, span)
        keep[0, :, span] = value[:half]
        encode(value[half:], R_DIR, span)

    unit_send(R_DIR, right)

    @columns
    def _(span):
        value = product(w, zl, tx, span)
        encode(value[:half], L_DIR, span)
        keep[1, :, span] = value[half:]

    unit_send(L_DIR, left)
    loss_next(1)
    loss_send(2)

    @columns
    def _(span):
        value = product(wt, 2 + i, im, span)
        encode(value[:half], Y_2, span)
        encode(value[half:], Y_3, span)

    unit_send(Y_2, p_same)
    unit_send(Y_3, p_same)

    @columns
    def _(span):
        value = product(wt, oi, im, span)
        keep[2, :, span] = value[:half]
        keep[3, :, span] = value[half:]

    loss_next(2)
    loss_send(3)

    def relay(got, kept, out, target):
        arrived(got)

        @columns
        def _(span):
            encode(keep[kept, :, span] + decode(got, span), out, span)

        unit_send(out, target)

    relay(F_R, 0, R_ACC, right)
    relay(F_L, 1, L_ACC, left)
    relay(Y_0, 2, X_0, across)
    relay(Y_1, 3, X_1, across)

    @columns
    def _(span):
        ig_ref[:, span] = product(w, z, tx, span)

    @columns
    def _(span):
        tg_ref[:, span] = product(wt, i, im, span)

    for k in range(3, len(flips)):
        loss_next(k)
        if k + 1 < len(flips):
            loss_send(k + 1)
    loss_ref[...] = loss_ref[...] / (2.0 * (n_blk * 8 * rows))

    def add(got, ref, where):
        arrived(got)

        @columns
        def _(span):
            ref[where, span] = ref[where, span] + decode(got, span)

    add(Y_2, tg_ref, lo)
    add(Y_3, tg_ref, hi)
    add(R_DIR, ig_ref, hi)
    add(L_DIR, ig_ref, lo)
    add(R_ACC, ig_ref, lo)
    add(L_ACC, ig_ref, hi)
    add(X_0, tg_ref, lo)
    add(X_1, tg_ref, hi)

    for copy in copies.values():
        copy.wait_send()


def shards(n_blk, images, texts, rest_row, rest_col):
    rows, width = images.shape
    tile = 4 * rows
    n_sum = 3 + (n_blk - 1).bit_length()
    vmem = pl.BlockSpec(memory_space=pltpu.VMEM)
    hbm = pl.BlockSpec(memory_space=pl.ANY)
    image_grad, text_grad, loss = pl.pallas_call(
        functools.partial(kernel, n_blk),
        out_shape=(
            jax.ShapeDtypeStruct((rows, width), F32),
            jax.ShapeDtypeStruct((rows, width), F32),
            jax.ShapeDtypeStruct((8, LANES), F32),
        ),
        in_specs=[hbm, hbm, vmem, vmem],
        out_specs=(vmem, vmem, vmem),
        scratch_shapes=[
            pltpu.VMEM((tile, width), BF16),
            pltpu.VMEM((tile, width), BF16),
            pltpu.VMEM((tile, tile), F32),
            pltpu.VMEM((tile, tile), BF16),
            pltpu.VMEM((tile, tile), BF16),
            pltpu.VMEM((tile, LANES), F32),
            pltpu.VMEM((32, tile), F32),
            pltpu.VMEM((32, tile), F32),
            pltpu.VMEM((8, tile), F32),
            pltpu.VMEM((4, 8, tile), F32),
            pltpu.VMEM((4, 8, 2 * rows), F32),
            pltpu.VMEM((4, 8, 2 * rows), F32),
            pltpu.VMEM((8, tile), F32),
            pltpu.VMEM((4, rows // 2, width), F32),
            pltpu.VMEM((UNITS, rows // 2 + PAD, width), BF16),
            pltpu.VMEM((UNITS, rows // 2 + PAD, width), BF16),
            pltpu.VMEM((n_sum, 8, LANES), F32),
            pltpu.VMEM((n_sum, 8, LANES), F32),
            pltpu.SemaphoreType.DMA((SUM + n_sum,)),
            pltpu.SemaphoreType.DMA((SUM + n_sum,)),
            pltpu.SemaphoreType.DMA((2,)),
        ],
        compiler_params=pltpu.CompilerParams(
            collective_id=0, has_side_effects=True, vmem_limit_bytes=60 << 20
        ),
        cost_estimate=pl.CostEstimate(
            flops=6 * tile * tile * width, bytes_accessed=8 * rows * width * 4, transcendentals=4 * tile * tile
        ),
    )(images, texts, rest_row[None, :], rest_col[None, :])
    return image_grad, text_grad, loss[0, 0]


def solution(mesh):
    return jax.shard_map(
        functools.partial(shards, mesh.shape["blk"]),
        mesh=mesh,
        in_specs=(
            P(("blk", "node"), None),
            P(("blk", "node"), None),
            P(("blk", "node")),
            P(("blk", "node")),
        ),
        out_specs=(P(("blk", "node"), None), P(("blk", "node"), None), P()),
        check_vma=False,
    )
```

```python
import functools

import jax
import jax.numpy as jnp
from jax import lax
from jax.experimental import pallas as pl
from jax.experimental.pallas import tpu as pltpu
from jax.sharding import PartitionSpec as P


MESH = pl.DeviceIdType.MESH
F32, BF16 = jnp.float32, jnp.bfloat16
logit_scale = 100.0
LANES = 128
CHUNK = 16
PAD = 16
WIDE = 256
POWER_RANGE = 2.0**18

(IMG_R0, IMG_R1, IMG_L1, IMG_L0, FWD_R, FWD_L, TXT_X0, TXT_X1, TXT_N0, TXT_N1, FWD_N0, FWD_N1) = range(12)
(ROW_R, ROW_L, ROW_F, OWN_X, OWN_NS, OWN_NO, PRV_X, PRV_PS, PRV_PO) = range(12, 21)
OUT = 21
(F_R, F_L, R_DIR, L_DIR, R_ACC, L_ACC, Y_0, Y_1, Y_2, Y_3, X_0, X_1) = range(12)
UNITS = 12
SUM = OUT + UNITS


def kernel(
    n_blk, img_ref, txt_ref, rr_ref, rc_ref, ig_ref, tg_ref, loss_ref,
    im, tx, s_ref, w, rowp, rows_s, colm, cols, rstat, rl, co, cp, cl, keep, acc, snd, rcv, lacc, lsnd, terms_ref,
    ss, rs, lsem,
):
    rows, width = img_ref.shape
    half = rows // 2
    tile = 4 * rows
    b = lax.axis_index("blk")
    node = lax.axis_index("node")
    i, z = node // 4, node % 4
    zr, zl, zf = (z + 1) % 4, (z + 3) % 4, (z + 2) % 4
    nxt, prv = (b + 1) % n_blk, (b + n_blk - 1) % n_blk
    oi = 1 - i

    def dev(blk, hi, zz):
        return (blk, hi * 4 + zz)

    right, left, far = dev(b, i, zr), dev(b, i, zl), dev(b, i, zf)
    across = dev(b, oi, z)
    n_same, n_other, p_same, p_other = dev(nxt, i, z), dev(nxt, oi, z), dev(prv, i, z), dev(prv, oi, z)

    def flip(value, step):
        return value + step - 2 * step * ((value // step) % 2)

    def flips(value, step, k):
        if k % 2:
            value = flip(value, step)
        return flip(value, 2 * step) if k // 2 else value

    blk_stages, step = [], 1
    while step < n_blk:
        count = min(4, n_blk // step)
        blk_stages.append((step, count))
        step *= count

    load_img = pltpu.make_async_copy(img_ref, im.at[pl.ds(pl.multiple_of(z * rows, rows), rows)], lsem.at[0])
    load_txt = pltpu.make_async_copy(txt_ref, tx.at[pl.ds(pl.multiple_of(i * rows, rows), rows)], lsem.at[1])
    load_img.start()
    load_txt.start()

    barrier = pltpu.get_barrier_semaphore()
    partners = [right, left, far, across, n_same, n_other, p_same, p_other]
    for step, count in blk_stages:
        partners += [dev(flips(b, step, k), i, z) for k in range(1, count) if step * k != 1]
    for partner in partners:
        pl.semaphore_signal(barrier, inc=1, device_id=partner, device_id_type=MESH)
    pl.semaphore_wait(barrier, len(partners))
    load_img.wait()
    load_txt.wait()

    def remote(k, src, dst, target):
        return pltpu.make_async_remote_copy(
            src_ref=src, dst_ref=dst, send_sem=ss.at[k], recv_sem=rs.at[k], device_id=target, device_id_type=MESH
        )

    def block(slot):
        return pl.ds(pl.multiple_of(slot * rows, rows), rows)

    def part(slot, h):
        return pl.ds(pl.multiple_of(slot * rows + h * half, half), half)

    copies = {}

    def send(k, src, dst, target):
        copies[k] = remote(k, src, dst, target)
        copies[k].start()

    def same(k, ref, where, target):
        send(k, ref.at[where], ref.at[where], target)

    odd = b % 2 == 1
    turn = b % 8 == 7

    def start(k, src, dst, target):
        copies[k] = remote(k, src, dst, target)
        return copies[k]

    same(IMG_R0, im, part(z, 0), right)
    same(IMG_L1, im, part(z, 1), left)
    own = [
        start(k, tx.at[part(i, h)], tx.at[part(2 + i, h)], n_same) for h, k in enumerate((TXT_N0, TXT_N1))
    ]

    @pl.when(jnp.logical_not(turn))
    def _():
        own[0].start()
        own[1].start()

    swap = [start(k, tx.at[part(i, h)], tx.at[part(i, h)], across) for h, k in enumerate((TXT_X0, TXT_X1))]

    swap[0].start()
    swap[1].start()

    same(IMG_R1, im, part(z, 1), right)
    same(IMG_L0, im, part(z, 0), left)
    slot = jnp.where(turn, i, oi)
    reach = dev(nxt, jnp.where(turn, oi, i), z)
    fwd = [
        start(k, tx.at[part(slot, h)], tx.at[part(2 + slot, h)], reach) for h, k in enumerate((FWD_N0, FWD_N1))
    ]

    def pick(t, *options):
        value = options[0]
        for k in range(1, len(options)):
            value = jnp.where(t == k, options[k], value)
        return value

    def logits_pair(q, p):
        pair = pl.ds(pl.multiple_of(p * 2 * rows, 2 * rows), 2 * rows)
        s_ref[block(q), pair] = logit_scale * lax.dot_general(
            im[block(q), :], tx[pair, :], (((1,), (1,)), ((), ())), preferred_element_type=F32
        )

    copies[IMG_R0].wait_recv()
    same(FWD_R, im, part(zl, 0), right)

    copies[IMG_L1].wait_recv()
    same(FWD_L, im, part(zr, 1), left)
    for h, k in enumerate((TXT_X0, TXT_X1)):
        copies[k].wait_recv()

        @pl.when(jnp.logical_not(turn))
        def _():
            fwd[h].start()

        @pl.when(turn)
        def _():
            if h == 0:
                for copy in own + fwd:
                    copy.start()

    n_chunks = rows // CHUNK
    n_lane = tile // LANES
    lanes = lambda k: pl.ds(k * LANES, LANES)

    def stats_pair(q, p, order):
        first = p * 2 * rows

        def lane(k):
            return pl.ds(pl.multiple_of(first + k * LANES, LANES), LANES)

        @pl.loop(0, n_chunks, unroll=4)
        def _(r):
            where = pl.ds(pl.multiple_of(q * rows + r * CHUNK, CHUNK), CHUNK)
            parts = [s_ref[where, lane(k)] for k in range(n_lane // 2)]
            top = functools.reduce(jnp.maximum, parts)
            rowp[p, where, :] = top
            rows_s[p, where, :] = functools.reduce(jnp.add, [jnp.exp(v - top) for v in parts])

        @pl.loop(0, n_lane // 2)
        def _(k):
            span = lane(k)
            parts = [s_ref[pl.ds(pl.multiple_of(q * rows + 8 * r, 8), 8), span] for r in range(rows // 8)]
            top = functools.reduce(jnp.maximum, parts)
            at = pl.ds(pl.multiple_of(order * 8, 8), 8)
            colm[at, span] = top
            cols[at, span] = functools.reduce(jnp.add, [jnp.exp(v - top) for v in parts])

    def row_stats(q):
        top = jnp.maximum(rowp[0, block(q), :], rowp[1, block(q), :])
        total = functools.reduce(
            jnp.add, [rows_s[p, block(q), :] * jnp.exp(rowp[p, block(q), :] - top) for p in range(2)]
        )
        top = jnp.transpose(top)
        best = jnp.max(top, axis=0, keepdims=True)
        total = jnp.sum(jnp.transpose(total) * jnp.exp(top - best), axis=0, keepdims=True)
        rstat[:, block(q)] = jnp.broadcast_to(best + jnp.log(total), (8, rows))

    copies[IMG_R1].wait_recv()
    copies[IMG_L0].wait_recv()

    @pl.loop(0, 3)
    def _(t):
        logits_pair(pick(t, z, zl, zr), 0)
        stats_pair(pick(t, z, zl, zr), 0, t)

    for k in (TXT_N0, TXT_N1, FWD_N0, FWD_N1):
        copies[k].wait_recv()

    @pl.loop(0, 3)
    def _(t):
        logits_pair(pick(t, z, zl, zr), 1)
        stats_pair(pick(t, z, zl, zr), 1, t)
        row_stats(pick(t, z, zl, zr))

    copies[FWD_R].wait_recv()
    copies[FWD_L].wait_recv()

    @pl.loop(0, 2)
    def _(p):
        logits_pair(zf, p)
        stats_pair(zf, p, 3)

    row_stats(zf)

    def join(a, c):
        top = jnp.maximum(a, c)
        return top + jnp.log(jnp.exp(a - top) + jnp.exp(c - top))

    rstat[:, block(z)] = join(rstat[:, block(z)], jnp.broadcast_to(rr_ref[...].reshape(1, rows), (8, rows)))
    rl[z] = rstat[...]
    for k, target in ((ROW_R, right), (ROW_L, left), (ROW_F, far)):
        send(k, rstat, rl.at[z], target)
    top = jnp.max(colm[...], axis=0, keepdims=True)
    total = jnp.sum(cols[...] * jnp.exp(colm[...] - top), axis=0, keepdims=True)
    both = jnp.broadcast_to(top + jnp.log(total), (8, tile))
    co[i] = both[:, : 2 * rows]
    cp[2 + i] = both[:, 2 * rows :]
    co[i, :, block(i)] = join(co[i, :, block(i)], jnp.broadcast_to(rc_ref[...].reshape(1, rows), (8, rows)))
    send(OWN_X, co.at[i], co.at[i], across)
    send(OWN_NS, co.at[i], cp.at[i], n_same)
    send(OWN_NO, co.at[i], cp.at[i], n_other)
    send(PRV_X, cp.at[2 + i], cp.at[2 + i], across)
    send(PRV_PS, cp.at[2 + i], co.at[2 + i], p_same)
    send(PRV_PO, cp.at[2 + i], co.at[2 + i], p_other)

    def diag_pass(r, total):
        s = s_ref[pl.ds(pl.multiple_of(z * rows + r * CHUNK, CHUNK), CHUNK), block(i)]
        row = lax.broadcasted_iota(jnp.int32, s.shape, 0) + r * CHUNK
        return total + jnp.where(lax.broadcasted_iota(jnp.int32, s.shape, 1) == row, s, 0.0)

    diag = jnp.sum(lax.fori_loop(0, n_chunks, diag_pass, jnp.zeros((CHUNK, rows), F32)), keepdims=True)

    def merged(parts):
        top = functools.reduce(jnp.maximum, parts)
        return top + jnp.log(functools.reduce(jnp.add, [jnp.exp(p - top) for p in parts]))

    for k in range(ROW_R, PRV_PO + 1):
        copies[k].wait_recv()
    cl[:, : 2 * rows] = merged([co[k] for k in range(4)])
    cl[:, 2 * rows :] = merged([cp[k] for k in range(4)])
    rstat2 = merged([rl[k] for k in range(4)])
    for q in range(4):
        column = jnp.broadcast_to(rstat2[0:1, q * rows : (q + 1) * rows], (LANES, rows))
        rowp[0, pl.ds(q * rows, rows), :] = jnp.transpose(column)

    terms = (
        jnp.sum(rowp[0, block(z), 0:1], keepdims=True)
        + jnp.sum(cl[0:1, block(i)], keepdims=True)
        - 2.0 * diag
    )
    lacc[...] = jnp.broadcast_to(terms, lacc.shape)
    stages = [(z, [right, left, far]), (i, [across])]
    for step, count in blk_stages:
        stages.append(((b // step) % count, [dev(flips(b, step, k), i, z) for k in range(1, count)]))
    first_message = [SUM + sum(len(t) for _, t in stages[:k]) for k in range(len(stages))]

    def loss_send(k):
        place, targets = stages[k]
        terms_ref[k, place] = lacc[...]
        lsnd[k] = lacc[...]
        for j, target in enumerate(targets):
            send(first_message[k] + j, lsnd.at[k], terms_ref.at[k, place], target)

    def loss_next(k):
        targets = stages[k][1]
        for j in range(len(targets)):
            copies[first_message[k] + j].wait_recv()
        lacc[...] = functools.reduce(jnp.add, [terms_ref[k, j] for j in range(len(targets) + 1)])

    def weights_block(q):
        mine = q == z

        @pl.loop(0, n_chunks)
        def _(r):
            where = pl.ds(pl.multiple_of(q * rows + r * CHUNK, CHUNK), CHUNK)
            row_lse = rowp[0, where, :]
            row = lax.broadcasted_iota(jnp.int32, (CHUNK, LANES), 0) + (r * CHUNK + i * rows)
            target = jnp.where(mine, row, -1) - lax.broadcasted_iota(jnp.int32, (CHUNK, LANES), 1)
            for k in range(n_lane):
                s = s_ref[where, lanes(k)]
                value = jnp.exp(s - row_lse) + jnp.exp(s - cl[0:1, lanes(k)])
                if k < n_lane // 2:
                    value = value - jnp.where(target == k * LANES, 2.0, 0.0)
                w[where, lanes(k)] = value.astype(BF16)

    def image_product(q, h):
        return logit_scale * jnp.dot(w[part(q, h), :], tx[...], preferred_element_type=F32)

    def text_product(t):
        return logit_scale * lax.dot_general(
            w[:, block(t)], im[...], (((0,), (0,)), ((), ())), preferred_element_type=F32
        )

    def encode(value, unit, span):
        top = jnp.maximum(jnp.max(jnp.abs(value), axis=0, keepdims=True), 1e-30)
        snd[unit, pl.ds(half, PAD), span] = jnp.broadcast_to(top, (PAD, WIDE)).astype(BF16)
        top = snd[unit, pl.ds(half, PAD), span].astype(F32)[0:1]
        u = value * (POWER_RANGE / top)
        u2 = u * u
        u4 = u2 * u2
        snd[unit, pl.ds(0, half), span] = (u4 * u2 * u).astype(BF16)

    def decode(unit, span):
        code = rcv[unit, pl.ds(0, half), span].astype(F32)
        top = rcv[unit, pl.ds(half, PAD), span].astype(F32)[0:1] * (1.0 / POWER_RANGE)
        size = jnp.abs(code)
        root = jnp.exp2(jnp.log2(size) * (1.0 / 7.0))
        return jnp.where(size > 0.0, jnp.where(code < 0.0, -root, root), 0.0) * top

    def unit_send(unit, target):
        send(OUT + unit, snd.at[unit], rcv.at[unit], target)

    def arrived(unit):
        copies[OUT + unit].wait_recv()

    def columns(body):
        @pl.loop(0, width // WIDE)
        def _(n):
            body(pl.ds(pl.multiple_of(n * WIDE, WIDE), WIDE))

    lo, hi = pl.ds(0, half), pl.ds(half, half)

    def encode_all(ref, where, unit):
        @columns
        def _(span):
            encode(ref[where, span], unit, span)

    loss_send(0)
    weights_block(zf)
    loss_next(0)
    loss_send(1)

    @pl.loop(0, 2)
    def _(u):
        acc[lo, :] = image_product(zf, u)
        encode_all(acc, lo, u)
        remote(OUT + u, snd.at[u], rcv.at[u], dev(b, i, pick(u, zr, zl))).start()

    loss_next(1)
    loss_send(2)

    @pl.loop(0, 3)
    def _(t):
        weights_block(pick(t, zr, zl, z))

    loss_next(2)
    loss_send(3)
    back_turn = b % 8 == 0
    y_first = dev(prv, jnp.where(back_turn, oi, i), z)

    @pl.loop(0, 3)
    def _(t):
        acc[...] = text_product(pick(t, 2 + oi, 2 + i, oi))

        @pl.when(t < 2)
        def _():
            target = dev(prv, pick(t, jnp.where(back_turn, oi, i), i), z)
            for h, where in enumerate((lo, hi)):
                unit = Y_0 + 2 * t + h
                encode_all(acc, where, unit)
                remote(OUT + unit, snd.at[unit], rcv.at[unit], target).start()

    def relay(got, kept, where, out):
        arrived(got)

        @columns
        def _(span):
            encode(kept[where, span] + decode(got, span), out, span)

    for unit, target in ((Y_0, y_first), (Y_1, y_first), (Y_2, p_same), (Y_3, p_same)):
        copies[OUT + unit] = remote(OUT + unit, snd.at[unit], rcv.at[unit], target)
    for unit in (X_0, X_1):
        copies[OUT + unit] = remote(OUT + unit, snd.at[unit], rcv.at[unit], across)

    def relay_text():
        for got, where, out in ((Y_0, lo, X_0), (Y_1, hi, X_1)):
            relay(got, acc, where, out)
            copies[OUT + out].start()

    @pl.when(jnp.logical_not(odd))
    def _():
        relay_text()

    @pl.when(turn)
    def _():
        for where, out in ((lo, X_0), (hi, X_1)):
            encode_all(acc, where, out)
            copies[OUT + out].start()

    @pl.loop(0, 4)
    def _(u):
        value = image_product(pick(u, zr, zl, zr, zl), pick(u, 1, 0, 0, 1))
        keep[pick(u, 2, 2, 0, 1)] = value

        @pl.when(u < 2)
        def _():
            encode_all(keep.at[2], slice(None), R_DIR + u)
            remote(
                OUT + R_DIR + u, snd.at[R_DIR + u], rcv.at[R_DIR + u], dev(b, i, pick(u, zr, zl))
            ).start()

    for unit, target in (
        (F_R, right), (F_L, left), (R_DIR, right), (L_DIR, left)
    ):
        copies[OUT + unit] = remote(OUT + unit, snd.at[unit], rcv.at[unit], target)

    @pl.when(jnp.logical_and(odd, jnp.logical_not(turn)))
    def _():
        relay_text()

    relay(F_R, keep.at[0], lo, R_ACC)
    unit_send(R_ACC, right)
    relay(F_L, keep.at[1], lo, L_ACC)
    unit_send(L_ACC, left)

    tg_ref[...] = text_product(i)

    @pl.loop(0, 2)
    def _(h):
        ig_ref[pl.ds(pl.multiple_of(h * half, half), half), :] = image_product(z, h)

    loss_next(3)
    loss_ref[...] = lacc[0:1, 0:1] / (2.0 * (n_blk * 8 * rows))

    def add(got, ref, where):
        arrived(got)

        @columns
        def _(span):
            ref[where, span] = ref[where, span] + decode(got, span)

    @pl.when(turn)
    def _():
        for got, where in ((Y_0, lo), (Y_1, hi)):
            add(got, tg_ref, where)

    add(Y_2, tg_ref, lo)
    add(Y_3, tg_ref, hi)
    add(R_DIR, ig_ref, hi)
    add(L_DIR, ig_ref, lo)
    add(R_ACC, ig_ref, lo)
    add(L_ACC, ig_ref, hi)
    add(X_0, tg_ref, lo)
    add(X_1, tg_ref, hi)

    for copy in copies.values():
        copy.wait_send()


def shards(n_blk, images, texts, rest_row, rest_col):
    rows, width = images.shape
    tile = 4 * rows
    n_stage, n_sum = 4, 3 + 1 + 3 + 3
    vmem = pl.BlockSpec(memory_space=pltpu.VMEM)
    hbm = pl.BlockSpec(memory_space=pl.ANY)
    image_grad, text_grad, loss = pl.pallas_call(
        functools.partial(kernel, n_blk),
        out_shape=(
            jax.ShapeDtypeStruct((rows, width), F32),
            jax.ShapeDtypeStruct((rows, width), F32),
            jax.ShapeDtypeStruct((1, 1), F32),
        ),
        in_specs=[hbm, hbm, vmem, vmem],
        out_specs=(vmem, vmem, vmem),
        scratch_shapes=[
            pltpu.VMEM((tile, width), BF16),
            pltpu.VMEM((tile, width), BF16),
            pltpu.VMEM((tile, tile), F32),
            pltpu.VMEM((tile, tile), BF16),
            pltpu.VMEM((2, tile, LANES), F32),
            pltpu.VMEM((2, tile, LANES), F32),
            pltpu.VMEM((32, tile), F32),
            pltpu.VMEM((32, tile), F32),
            pltpu.VMEM((8, tile), F32),
            pltpu.VMEM((4, 8, tile), F32),
            pltpu.VMEM((4, 8, 2 * rows), F32),
            pltpu.VMEM((4, 8, 2 * rows), F32),
            pltpu.VMEM((8, tile), F32),
            pltpu.VMEM((3, rows // 2, width), F32),
            pltpu.VMEM((rows, width), F32),
            pltpu.VMEM((UNITS, rows // 2 + PAD, width), BF16),
            pltpu.VMEM((UNITS, rows // 2 + PAD, width), BF16),
            pltpu.VMEM((8, LANES), F32),
            pltpu.VMEM((n_stage, 8, LANES), F32),
            pltpu.VMEM((n_stage, 4, 8, LANES), F32),
            pltpu.SemaphoreType.DMA((SUM + n_sum,)),
            pltpu.SemaphoreType.DMA((SUM + n_sum,)),
            pltpu.SemaphoreType.DMA((2,)),
        ],
        compiler_params=pltpu.CompilerParams(
            collective_id=0, has_side_effects=True, vmem_limit_bytes=60 << 20
        ),
        cost_estimate=pl.CostEstimate(
            flops=6 * tile * tile * width, bytes_accessed=8 * rows * width * 4, transcendentals=4 * tile * tile
        ),
    )(images, texts, rest_row, rest_col)
    return image_grad, text_grad, loss.reshape(())


def solution(mesh):
    return jax.shard_map(
        functools.partial(shards, mesh.shape["blk"]),
        mesh=mesh,
        in_specs=(
            P(("blk", "node"), None),
            P(("blk", "node"), None),
            P(("blk", "node")),
            P(("blk", "node")),
        ),
        out_specs=(P(("blk", "node"), None), P(("blk", "node"), None), P()),
        check_vma=False,
    )
```

```python
import functools

import jax
import jax.numpy as jnp
from jax import lax
from jax.experimental import pallas as pl
from jax.experimental.pallas import tpu as pltpu
from jax.sharding import PartitionSpec as P


MESH = pl.DeviceIdType.MESH
F32, BF16 = jnp.float32, jnp.bfloat16
logit_scale = 100.0
LANES = 128
CHUNK = 16
PAD = 16
WIDE = 256
POWER_RANGE = 2.0**18

(IMG_R0, IMG_R1, IMG_L1, IMG_L0, FWD_R, FWD_L, TXT_X0, TXT_X1, TXT_N0, TXT_N1, FWD_N0, FWD_N1) = range(12)
(ROW_R, ROW_L, ROW_F, OWN_X, OWN_NS, OWN_NO, PRV_X, PRV_PS, PRV_PO) = range(12, 21)
(VIA_0, VIA_1, VIA_S0, VIA_S1, VIA_O0, VIA_O1) = range(21, 27)
OUT = 27
(F_R, F_L, R_DIR, L_DIR, R_ACC, L_ACC, Y_0, Y_1, Y_2, Y_3, X_0, X_1) = range(12)
UNITS = 12
SUM = OUT + UNITS


def kernel(
    n_blk, img_ref, txt_ref, rr_ref, rc_ref, ig_ref, tg_ref, loss_ref,
    im, tx, s_ref, w, rowp, rows_s, colm, cols, rstat, rl, co, cp, cl, keep, acc, via, snd, rcv, lacc, lsnd, terms_ref,
    ss, rs, lsem,
):
    rows, width = img_ref.shape
    half = rows // 2
    tile = 4 * rows
    b = lax.axis_index("blk")
    node = lax.axis_index("node")
    i, z = node // 4, node % 4
    zr, zl, zf = (z + 1) % 4, (z + 3) % 4, (z + 2) % 4
    nxt, prv = (b + 1) % n_blk, (b + n_blk - 1) % n_blk
    oi = 1 - i

    def dev(blk, hi, zz):
        return (blk, hi * 4 + zz)

    right, left, far = dev(b, i, zr), dev(b, i, zl), dev(b, i, zf)
    across = dev(b, oi, z)
    n_same, n_other, p_same, p_other = dev(nxt, i, z), dev(nxt, oi, z), dev(prv, i, z), dev(prv, oi, z)

    def flip(value, step):
        return value + step - 2 * step * ((value // step) % 2)

    def flips(value, step, k):
        if k % 2:
            value = flip(value, step)
        return flip(value, 2 * step) if k // 2 else value

    blk_stages, step = [], 1
    while step < n_blk:
        count = min(4, n_blk // step)
        blk_stages.append((step, count))
        step *= count

    load_img = pltpu.make_async_copy(img_ref, im.at[pl.ds(pl.multiple_of(z * rows, rows), rows)], lsem.at[0])
    load_txt = pltpu.make_async_copy(txt_ref, tx.at[pl.ds(pl.multiple_of(i * rows, rows), rows)], lsem.at[1])
    load_img.start()
    load_txt.start()

    barrier = pltpu.get_barrier_semaphore()
    partners = [right, left, far, across, n_same, n_other, p_same, p_other]
    for step, count in blk_stages:
        partners += [dev(flips(b, step, k), i, z) for k in range(1, count) if step * k != 1]
    for partner in partners:
        pl.semaphore_signal(barrier, inc=1, device_id=partner, device_id_type=MESH)

    turn, between, ahead = b % 8 == 7, b % 8 == 1, b % 8 == 0
    via_dev = dev((b + n_blk - 6) % n_blk, i, z)
    via_from = dev((b + 6) % n_blk, i, z)
    via_same, via_other = dev((b + 7) % n_blk, i, z), dev((b + 7) % n_blk, oi, z)
    from_same, from_other = dev((b + n_blk - 7) % n_blk, i, z), dev((b + n_blk - 7) % n_blk, oi, z)
    for role, others in (
        (turn, [via_dev]), (between, [via_from, via_same, via_other]), (ahead, [from_same, from_other])
    ):

        @pl.when(role)
        def _():
            for partner in others:
                pl.semaphore_signal(barrier, inc=1, device_id=partner, device_id_type=MESH)

    extra = jnp.where(turn, 1, 0) + jnp.where(between, 3, 0) + jnp.where(ahead, 2, 0)
    pl.semaphore_wait(barrier, len(partners) + extra)
    load_img.wait()
    load_txt.wait()

    def remote(k, src, dst, target):
        return pltpu.make_async_remote_copy(
            src_ref=src, dst_ref=dst, send_sem=ss.at[k], recv_sem=rs.at[k], device_id=target, device_id_type=MESH
        )

    def block(slot):
        return pl.ds(pl.multiple_of(slot * rows, rows), rows)

    def part(slot, h):
        return pl.ds(pl.multiple_of(slot * rows + h * half, half), half)

    copies = {}

    def send(k, src, dst, target):
        copies[k] = remote(k, src, dst, target)
        copies[k].start()

    def same(k, ref, where, target):
        send(k, ref.at[where], ref.at[where], target)

    odd = b % 2 == 1

    def start(k, src, dst, target):
        copies[k] = remote(k, src, dst, target)
        return copies[k]

    same(IMG_R0, im, part(z, 0), right)
    same(IMG_L1, im, part(z, 1), left)
    own = [
        start(k, tx.at[part(i, h)], tx.at[part(2 + i, h)], n_same) for h, k in enumerate((TXT_N0, TXT_N1))
    ]

    via_in = [start(k, tx.at[part(i, h)], via.at[pl.ds(h * half, half)], via_dev) for h, k in enumerate((VIA_0, VIA_1))]
    via_out = [
        pltpu.make_async_remote_copy(
            src_ref=via.at[pl.ds(h * half, half)],
            dst_ref=tx.at[part(2 + i, h)],
            send_sem=ss.at[k],
            recv_sem=rs.at[landing],
            device_id=target,
            device_id_type=MESH,
        )
        for h, k, landing, target in (
            (0, VIA_S0, TXT_N0, via_same), (0, VIA_O0, FWD_N0, via_other),
            (1, VIA_S1, TXT_N1, via_same), (1, VIA_O1, FWD_N1, via_other),
        )
    ]

    @pl.when(turn)
    def _():
        via_in[0].start()
        via_in[1].start()

    @pl.when(jnp.logical_not(turn))
    def _():
        own[0].start()
        own[1].start()

    swap = [start(k, tx.at[part(i, h)], tx.at[part(i, h)], across) for h, k in enumerate((TXT_X0, TXT_X1))]

    swap[0].start()
    swap[1].start()

    same(IMG_R1, im, part(z, 1), right)
    same(IMG_L0, im, part(z, 0), left)
    fwd = [
        start(k, tx.at[part(oi, h)], tx.at[part(2 + oi, h)], n_same) for h, k in enumerate((FWD_N0, FWD_N1))
    ]

    def pick(t, *options):
        value = options[0]
        for k in range(1, len(options)):
            value = jnp.where(t == k, options[k], value)
        return value

    def logits_pair(q, p):
        pair = pl.ds(pl.multiple_of(p * 2 * rows, 2 * rows), 2 * rows)
        s_ref[block(q), pair] = logit_scale * lax.dot_general(
            im[block(q), :], tx[pair, :], (((1,), (1,)), ((), ())), preferred_element_type=F32
        )

    @pl.when(between)
    def _():
        for h in range(2):
            via_in[h].wait_recv()
            via_out[2 * h].start()
            via_out[2 * h + 1].start()

    copies[IMG_R0].wait_recv()
    same(FWD_R, im, part(zl, 0), right)

    copies[IMG_L1].wait_recv()
    same(FWD_L, im, part(zr, 1), left)
    for h, k in enumerate((TXT_X0, TXT_X1)):
        copies[k].wait_recv()

        @pl.when(jnp.logical_not(turn))
        def _():
            fwd[h].start()

    n_chunks = rows // CHUNK
    n_lane = tile // LANES
    lanes = lambda k: pl.ds(k * LANES, LANES)

    def stats_pair(q, p, order):
        first = p * 2 * rows

        def lane(k):
            return pl.ds(pl.multiple_of(first + k * LANES, LANES), LANES)

        @pl.loop(0, n_chunks, unroll=4)
        def _(r):
            where = pl.ds(pl.multiple_of(q * rows + r * CHUNK, CHUNK), CHUNK)
            parts = [s_ref[where, lane(k)] for k in range(n_lane // 2)]
            top = functools.reduce(jnp.maximum, parts)
            rowp[p, where, :] = top
            rows_s[p, where, :] = functools.reduce(jnp.add, [jnp.exp(v - top) for v in parts])

        @pl.loop(0, n_lane // 2)
        def _(k):
            span = lane(k)
            parts = [s_ref[pl.ds(pl.multiple_of(q * rows + 8 * r, 8), 8), span] for r in range(rows // 8)]
            top = functools.reduce(jnp.maximum, parts)
            at = pl.ds(pl.multiple_of(order * 8, 8), 8)
            colm[at, span] = top
            cols[at, span] = functools.reduce(jnp.add, [jnp.exp(v - top) for v in parts])

    def row_stats(q):
        top = jnp.maximum(rowp[0, block(q), :], rowp[1, block(q), :])
        total = functools.reduce(
            jnp.add, [rows_s[p, block(q), :] * jnp.exp(rowp[p, block(q), :] - top) for p in range(2)]
        )
        top = jnp.transpose(top)
        best = jnp.max(top, axis=0, keepdims=True)
        total = jnp.sum(jnp.transpose(total) * jnp.exp(top - best), axis=0, keepdims=True)
        rstat[:, block(q)] = jnp.broadcast_to(best + jnp.log(total), (8, rows))

    copies[IMG_R1].wait_recv()
    copies[IMG_L0].wait_recv()

    @pl.loop(0, 3)
    def _(t):
        logits_pair(pick(t, z, zl, zr), 0)
        stats_pair(pick(t, z, zl, zr), 0, t)

    for k in (TXT_N0, TXT_N1, FWD_N0, FWD_N1):
        copies[k].wait_recv()

    @pl.loop(0, 3)
    def _(t):
        logits_pair(pick(t, z, zl, zr), 1)
        stats_pair(pick(t, z, zl, zr), 1, t)
        row_stats(pick(t, z, zl, zr))

    copies[FWD_R].wait_recv()
    copies[FWD_L].wait_recv()

    @pl.loop(0, 2)
    def _(p):
        logits_pair(zf, p)
        stats_pair(zf, p, 3)

    row_stats(zf)

    def join(a, c):
        top = jnp.maximum(a, c)
        return top + jnp.log(jnp.exp(a - top) + jnp.exp(c - top))

    rstat[:, block(z)] = join(rstat[:, block(z)], jnp.broadcast_to(rr_ref[...].reshape(1, rows), (8, rows)))
    rl[z] = rstat[...]
    for k, target in ((ROW_R, right), (ROW_L, left), (ROW_F, far)):
        send(k, rstat, rl.at[z], target)
    top = jnp.max(colm[...], axis=0, keepdims=True)
    total = jnp.sum(cols[...] * jnp.exp(colm[...] - top), axis=0, keepdims=True)
    both = jnp.broadcast_to(top + jnp.log(total), (8, tile))
    co[i] = both[:, : 2 * rows]
    cp[2 + i] = both[:, 2 * rows :]
    co[i, :, block(i)] = join(co[i, :, block(i)], jnp.broadcast_to(rc_ref[...].reshape(1, rows), (8, rows)))
    send(OWN_X, co.at[i], co.at[i], across)
    send(OWN_NS, co.at[i], cp.at[i], n_same)
    send(OWN_NO, co.at[i], cp.at[i], n_other)
    send(PRV_X, cp.at[2 + i], cp.at[2 + i], across)
    send(PRV_PS, cp.at[2 + i], co.at[2 + i], p_same)
    send(PRV_PO, cp.at[2 + i], co.at[2 + i], p_other)

    def diag_pass(r, total):
        s = s_ref[pl.ds(pl.multiple_of(z * rows + r * CHUNK, CHUNK), CHUNK), block(i)]
        row = lax.broadcasted_iota(jnp.int32, s.shape, 0) + r * CHUNK
        return total + jnp.where(lax.broadcasted_iota(jnp.int32, s.shape, 1) == row, s, 0.0)

    diag = jnp.sum(lax.fori_loop(0, n_chunks, diag_pass, jnp.zeros((CHUNK, rows), F32)), keepdims=True)

    def merged(parts):
        top = functools.reduce(jnp.maximum, parts)
        return top + jnp.log(functools.reduce(jnp.add, [jnp.exp(p - top) for p in parts]))

    for k in range(ROW_R, PRV_PO + 1):
        copies[k].wait_recv()
    cl[:, : 2 * rows] = merged([co[k] for k in range(4)])
    cl[:, 2 * rows :] = merged([cp[k] for k in range(4)])
    rstat2 = merged([rl[k] for k in range(4)])
    for q in range(4):
        column = jnp.broadcast_to(rstat2[0:1, q * rows : (q + 1) * rows], (LANES, rows))
        rowp[0, pl.ds(q * rows, rows), :] = jnp.transpose(column)

    terms = (
        jnp.sum(rowp[0, block(z), 0:1], keepdims=True)
        + jnp.sum(cl[0:1, block(i)], keepdims=True)
        - 2.0 * diag
    )
    lacc[...] = jnp.broadcast_to(terms, lacc.shape)
    stages = [(z, [right, left, far]), (i, [across])]
    for step, count in blk_stages:
        stages.append(((b // step) % count, [dev(flips(b, step, k), i, z) for k in range(1, count)]))
    first_message = [SUM + sum(len(t) for _, t in stages[:k]) for k in range(len(stages))]

    def loss_send(k):
        place, targets = stages[k]
        terms_ref[k, place] = lacc[...]
        lsnd[k] = lacc[...]
        for j, target in enumerate(targets):
            send(first_message[k] + j, lsnd.at[k], terms_ref.at[k, place], target)

    def loss_next(k):
        targets = stages[k][1]
        for j in range(len(targets)):
            copies[first_message[k] + j].wait_recv()
        lacc[...] = functools.reduce(jnp.add, [terms_ref[k, j] for j in range(len(targets) + 1)])

    def weights_block(q):
        mine = q == z

        @pl.loop(0, n_chunks)
        def _(r):
            where = pl.ds(pl.multiple_of(q * rows + r * CHUNK, CHUNK), CHUNK)
            row_lse = rowp[0, where, :]
            row = lax.broadcasted_iota(jnp.int32, (CHUNK, LANES), 0) + (r * CHUNK + i * rows)
            target = jnp.where(mine, row, -1) - lax.broadcasted_iota(jnp.int32, (CHUNK, LANES), 1)
            for k in range(n_lane):
                s = s_ref[where, lanes(k)]
                value = jnp.exp(s - row_lse) + jnp.exp(s - cl[0:1, lanes(k)])
                if k < n_lane // 2:
                    value = value - jnp.where(target == k * LANES, 2.0, 0.0)
                w[where, lanes(k)] = value.astype(BF16)

    def image_product(q, h):
        return logit_scale * jnp.dot(w[part(q, h), :], tx[...], preferred_element_type=F32)

    def text_product(t):
        return logit_scale * lax.dot_general(
            w[:, block(t)], im[...], (((0,), (0,)), ((), ())), preferred_element_type=F32
        )

    def encode(value, unit, span):
        top = jnp.maximum(jnp.max(jnp.abs(value), axis=0, keepdims=True), 1e-30)
        snd[unit, pl.ds(half, PAD), span] = jnp.broadcast_to(top, (PAD, WIDE)).astype(BF16)
        top = snd[unit, pl.ds(half, PAD), span].astype(F32)[0:1]
        u = value * (POWER_RANGE / top)
        u2 = u * u
        u4 = u2 * u2
        snd[unit, pl.ds(0, half), span] = (u4 * u2 * u).astype(BF16)

    def decode(unit, span):
        code = rcv[unit, pl.ds(0, half), span].astype(F32)
        top = rcv[unit, pl.ds(half, PAD), span].astype(F32)[0:1] * (1.0 / POWER_RANGE)
        size = jnp.abs(code)
        root = jnp.exp2(jnp.log2(size) * (1.0 / 7.0))
        return jnp.where(size > 0.0, jnp.where(code < 0.0, -root, root), 0.0) * top

    def unit_send(unit, target):
        send(OUT + unit, snd.at[unit], rcv.at[unit], target)

    def arrived(unit):
        copies[OUT + unit].wait_recv()

    def columns(body):
        @pl.loop(0, width // WIDE)
        def _(n):
            body(pl.ds(pl.multiple_of(n * WIDE, WIDE), WIDE))

    lo, hi = pl.ds(0, half), pl.ds(half, half)

    def encode_all(ref, where, unit):
        @columns
        def _(span):
            encode(ref[where, span], unit, span)

    loss_send(0)
    weights_block(zf)
    loss_next(0)
    loss_send(1)

    @pl.loop(0, 2)
    def _(u):
        acc[lo, :] = image_product(zf, u)
        encode_all(acc, lo, u)
        remote(OUT + u, snd.at[u], rcv.at[u], dev(b, i, pick(u, zr, zl))).start()

    loss_next(1)
    loss_send(2)

    @pl.loop(0, 3)
    def _(t):
        weights_block(pick(t, zr, zl, z))

    back_turn = b % 8 == 0
    y_first = dev(prv, jnp.where(back_turn, oi, i), z)

    def relay(got, kept, where, out):
        arrived(got)

        @columns
        def _(span):
            encode(kept[where, span] + decode(got, span), out, span)

    for unit, target in ((Y_0, y_first), (Y_1, y_first), (Y_2, p_same), (Y_3, p_same)):
        copies[OUT + unit] = remote(OUT + unit, snd.at[unit], rcv.at[unit], target)
    for unit in (X_0, X_1):
        copies[OUT + unit] = remote(OUT + unit, snd.at[unit], rcv.at[unit], across)

    def relay_text():
        for got, where, out in ((Y_0, lo, X_0), (Y_1, hi, X_1)):
            relay(got, acc, where, out)
            copies[OUT + out].start()

    @pl.loop(0, 3)
    def _(t):
        slot = jnp.where(back_turn, pick(t, oi, 2 + oi, 2 + i), pick(t, 2 + oi, 2 + i, oi))
        acc[...] = text_product(slot)

        @pl.when(jnp.logical_and(back_turn, t == 0))
        def _():
            relay_text()

        @pl.when(slot >= 2)
        def _():
            turned = t - jnp.where(back_turn, 1, 0)
            target = dev(prv, pick(turned, jnp.where(back_turn, oi, i), i), z)
            for h, where in enumerate((lo, hi)):
                unit = Y_0 + 2 * turned + h
                encode_all(acc, where, unit)
                remote(OUT + unit, snd.at[unit], rcv.at[unit], target).start()

    @pl.when(jnp.logical_not(jnp.logical_or(odd, back_turn)))
    def _():
        relay_text()

    @pl.when(turn)
    def _():
        for where, out in ((lo, X_0), (hi, X_1)):
            encode_all(acc, where, out)
            copies[OUT + out].start()

    @pl.loop(0, 4)
    def _(u):
        value = image_product(pick(u, zr, zl, zr, zl), pick(u, 1, 0, 0, 1))
        keep[pick(u, 2, 2, 0, 1)] = value

        @pl.when(u < 2)
        def _():
            encode_all(keep.at[2], slice(None), R_DIR + u)
            remote(
                OUT + R_DIR + u, snd.at[R_DIR + u], rcv.at[R_DIR + u], dev(b, i, pick(u, zr, zl))
            ).start()

    for unit, target in (
        (F_R, right), (F_L, left), (R_DIR, right), (L_DIR, left)
    ):
        copies[OUT + unit] = remote(OUT + unit, snd.at[unit], rcv.at[unit], target)

    @pl.when(jnp.logical_and(odd, jnp.logical_not(turn)))
    def _():
        relay_text()

    loss_next(2)
    loss_send(3)
    relay(F_R, keep.at[0], lo, R_ACC)
    unit_send(R_ACC, right)
    relay(F_L, keep.at[1], lo, L_ACC)
    unit_send(L_ACC, left)

    tg_ref[...] = text_product(i)

    @pl.loop(0, 2)
    def _(h):
        ig_ref[pl.ds(pl.multiple_of(h * half, half), half), :] = image_product(z, h)

    loss_next(3)
    loss_ref[...] = lacc[0:1, 0:1] / (2.0 * (n_blk * 8 * rows))

    def add(got, ref, where):
        arrived(got)

        @columns
        def _(span):
            ref[where, span] = ref[where, span] + decode(got, span)

    @pl.when(turn)
    def _():
        for got, where in ((Y_0, lo), (Y_1, hi)):
            add(got, tg_ref, where)

    add(Y_2, tg_ref, lo)
    add(Y_3, tg_ref, hi)
    add(R_DIR, ig_ref, hi)
    add(L_DIR, ig_ref, lo)
    add(R_ACC, ig_ref, lo)
    add(L_ACC, ig_ref, hi)
    add(X_0, tg_ref, lo)
    add(X_1, tg_ref, hi)

    for k, copy in copies.items():
        if k not in (TXT_N0, TXT_N1, FWD_N0, FWD_N1, VIA_0, VIA_1):
            copy.wait_send()
    for role, sent in ((turn, via_in), (between, via_out), (jnp.logical_not(turn), own + fwd)):

        @pl.when(role)
        def _():
            for copy in sent:
                copy.wait_send()


def shards(n_blk, images, texts, rest_row, rest_col):
    rows, width = images.shape
    tile = 4 * rows
    n_stage, n_sum = 4, 3 + 1 + 3 + 3
    vmem = pl.BlockSpec(memory_space=pltpu.VMEM)
    hbm = pl.BlockSpec(memory_space=pl.ANY)
    image_grad, text_grad, loss = pl.pallas_call(
        functools.partial(kernel, n_blk),
        out_shape=(
            jax.ShapeDtypeStruct((rows, width), F32),
            jax.ShapeDtypeStruct((rows, width), F32),
            jax.ShapeDtypeStruct((1, 1), F32),
        ),
        in_specs=[hbm, hbm, vmem, vmem],
        out_specs=(vmem, vmem, vmem),
        scratch_shapes=[
            pltpu.VMEM((tile, width), BF16),
            pltpu.VMEM((tile, width), BF16),
            pltpu.VMEM((tile, tile), F32),
            pltpu.VMEM((tile, tile), BF16),
            pltpu.VMEM((2, tile, LANES), F32),
            pltpu.VMEM((2, tile, LANES), F32),
            pltpu.VMEM((32, tile), F32),
            pltpu.VMEM((32, tile), F32),
            pltpu.VMEM((8, tile), F32),
            pltpu.VMEM((4, 8, tile), F32),
            pltpu.VMEM((4, 8, 2 * rows), F32),
            pltpu.VMEM((4, 8, 2 * rows), F32),
            pltpu.VMEM((8, tile), F32),
            pltpu.VMEM((3, rows // 2, width), F32),
            pltpu.VMEM((rows, width), F32),
            pltpu.VMEM((rows, width), BF16),
            pltpu.VMEM((UNITS, rows // 2 + PAD, width), BF16),
            pltpu.VMEM((UNITS, rows // 2 + PAD, width), BF16),
            pltpu.VMEM((8, LANES), F32),
            pltpu.VMEM((n_stage, 8, LANES), F32),
            pltpu.VMEM((n_stage, 4, 8, LANES), F32),
            pltpu.SemaphoreType.DMA((SUM + n_sum,)),
            pltpu.SemaphoreType.DMA((SUM + n_sum,)),
            pltpu.SemaphoreType.DMA((2,)),
        ],
        compiler_params=pltpu.CompilerParams(
            collective_id=0, has_side_effects=True, vmem_limit_bytes=60 << 20
        ),
        cost_estimate=pl.CostEstimate(
            flops=6 * tile * tile * width, bytes_accessed=8 * rows * width * 4, transcendentals=4 * tile * tile
        ),
    )(images, texts, rest_row, rest_col)
    return image_grad, text_grad, loss.reshape(())


def solution(mesh):
    return jax.shard_map(
        functools.partial(shards, mesh.shape["blk"]),
        mesh=mesh,
        in_specs=(
            P(("blk", "node"), None),
            P(("blk", "node"), None),
            P(("blk", "node")),
            P(("blk", "node")),
        ),
        out_specs=(P(("blk", "node"), None), P(("blk", "node"), None), P()),
        check_vma=False,
    )
```

```python
import functools

import jax
import jax.numpy as jnp
from jax import lax
from jax.experimental import pallas as pl
from jax.experimental.pallas import tpu as pltpu
from jax.sharding import PartitionSpec as P


MESH = pl.DeviceIdType.MESH
F32, BF16 = jnp.float32, jnp.bfloat16
logit_scale = 100.0
LANES = 128
CHUNK = 16
PAD = 16
WIDE = 256
POWER_RANGE = 2.0**18

(IMG_R0, IMG_R1, IMG_L1, IMG_L0, FWD_R, FWD_L, TXT_X0, TXT_X1, TXT_N0, TXT_N1, FWD_N0, FWD_N1) = range(12)
(ROW_R, ROW_L, ROW_F, OWN_X, OWN_NS, OWN_NO, PRV_X, PRV_PS, PRV_PO) = range(12, 21)
(VIA_0, VIA_1, VIA_S0, VIA_S1, VIA_O0, VIA_O1) = range(21, 27)
(BACK_0, BACK_1) = range(27, 29)
OUT = 29
(F_R, F_L, R_DIR, L_DIR, R_ACC, L_ACC, Y_0, Y_1, Y_2, Y_3, X_0, X_1) = range(12)
UNITS = 12
SUM = OUT + UNITS


def kernel(
    n_blk, img_ref, txt_ref, rr_ref, rc_ref, ig_ref, tg_ref, loss_ref,
    im, tx, s_ref, w, rowp, rows_s, colm, cols, rstat, rl, co, cp, cl, keep, acc, via, bk, snd, rcv, lacc, lsnd, terms_ref,
    ss, rs, lsem,
):
    rows, width = img_ref.shape
    half = rows // 2
    tile = 4 * rows
    b = lax.axis_index("blk")
    node = lax.axis_index("node")
    i, z = node // 4, node % 4
    zr, zl, zf = (z + 1) % 4, (z + 3) % 4, (z + 2) % 4
    nxt, prv = (b + 1) % n_blk, (b + n_blk - 1) % n_blk
    oi = 1 - i

    def dev(blk, hi, zz):
        return (blk, hi * 4 + zz)

    right, left, far = dev(b, i, zr), dev(b, i, zl), dev(b, i, zf)
    across = dev(b, oi, z)
    n_same, n_other, p_same, p_other = dev(nxt, i, z), dev(nxt, oi, z), dev(prv, i, z), dev(prv, oi, z)

    def flip(value, step):
        return value + step - 2 * step * ((value // step) % 2)

    def flips(value, step, k):
        if k % 2:
            value = flip(value, step)
        return flip(value, 2 * step) if k // 2 else value

    blk_stages, step = [], 1
    while step < n_blk:
        count = min(4, n_blk // step)
        blk_stages.append((step, count))
        step *= count

    load_img = pltpu.make_async_copy(img_ref, im.at[pl.ds(pl.multiple_of(z * rows, rows), rows)], lsem.at[0])
    load_txt = pltpu.make_async_copy(txt_ref, tx.at[pl.ds(pl.multiple_of(i * rows, rows), rows)], lsem.at[1])
    load_img.start()
    load_txt.start()

    barrier = pltpu.get_barrier_semaphore()
    partners = [right, left, far, across, n_same, n_other, p_same, p_other]
    for step, count in blk_stages:
        partners += [dev(flips(b, step, k), i, z) for k in range(1, count) if step * k != 1]
    for partner in partners:
        pl.semaphore_signal(barrier, inc=1, device_id=partner, device_id_type=MESH)

    turn, between, ahead = b % 8 == 7, b % 8 == 1, b % 8 == 0
    via_dev = dev((b + n_blk - 6) % n_blk, i, z)
    via_from = dev((b + 6) % n_blk, i, z)
    via_same, via_other = dev((b + 7) % n_blk, i, z), dev((b + 7) % n_blk, oi, z)
    from_same, from_other = dev((b + n_blk - 7) % n_blk, i, z), dev((b + n_blk - 7) % n_blk, oi, z)
    backer = b % 8 == 6
    back_dev, back_src = dev((b + 6) % n_blk, i, z), dev((b + 7) % n_blk, i, z)
    back_from, back_to = dev((b + n_blk - 6) % n_blk, i, z), dev((b + n_blk - 7) % n_blk, i, z)
    for role, others in (
        (turn, [via_dev, back_src]),
        (between, [via_from, via_same, via_other]),
        (ahead, [from_same, from_other, back_dev]),
        (backer, [back_from, back_to]),
    ):

        @pl.when(role)
        def _():
            for partner in others:
                pl.semaphore_signal(barrier, inc=1, device_id=partner, device_id_type=MESH)

    extra = jnp.where(turn, 2, 0) + jnp.where(between, 3, 0) + jnp.where(ahead, 3, 0) + jnp.where(backer, 2, 0)
    pl.semaphore_wait(barrier, len(partners) + extra)
    load_img.wait()
    load_txt.wait()

    def remote(k, src, dst, target):
        return pltpu.make_async_remote_copy(
            src_ref=src, dst_ref=dst, send_sem=ss.at[k], recv_sem=rs.at[k], device_id=target, device_id_type=MESH
        )

    def block(slot):
        return pl.ds(pl.multiple_of(slot * rows, rows), rows)

    def part(slot, h):
        return pl.ds(pl.multiple_of(slot * rows + h * half, half), half)

    copies = {}

    def send(k, src, dst, target):
        copies[k] = remote(k, src, dst, target)
        copies[k].start()

    def same(k, ref, where, target):
        send(k, ref.at[where], ref.at[where], target)

    odd = b % 2 == 1

    def start(k, src, dst, target):
        copies[k] = remote(k, src, dst, target)
        return copies[k]

    same(IMG_R0, im, part(z, 0), right)
    same(IMG_L1, im, part(z, 1), left)
    own = [
        start(k, tx.at[part(i, h)], tx.at[part(2 + i, h)], n_same) for h, k in enumerate((TXT_N0, TXT_N1))
    ]

    via_in = [start(k, tx.at[part(i, h)], via.at[pl.ds(h * half, half)], via_dev) for h, k in enumerate((VIA_0, VIA_1))]
    via_out = [
        pltpu.make_async_remote_copy(
            src_ref=via.at[pl.ds(h * half, half)],
            dst_ref=tx.at[part(2 + i, h)],
            send_sem=ss.at[k],
            recv_sem=rs.at[landing],
            device_id=target,
            device_id_type=MESH,
        )
        for h, k, landing, target in (
            (0, VIA_S0, TXT_N0, via_same), (0, VIA_O0, FWD_N0, via_other),
            (1, VIA_S1, TXT_N1, via_same), (1, VIA_O1, FWD_N1, via_other),
        )
    ]

    @pl.when(turn)
    def _():
        via_in[0].start()
        via_in[1].start()

    @pl.when(jnp.logical_not(turn))
    def _():
        own[0].start()
        own[1].start()

    swap = [start(k, tx.at[part(i, h)], tx.at[part(i, h)], across) for h, k in enumerate((TXT_X0, TXT_X1))]

    swap[0].start()
    swap[1].start()

    same(IMG_R1, im, part(z, 1), right)
    same(IMG_L0, im, part(z, 0), left)
    fwd = [
        start(k, tx.at[part(oi, h)], tx.at[part(2 + oi, h)], n_same) for h, k in enumerate((FWD_N0, FWD_N1))
    ]

    def pick(t, *options):
        value = options[0]
        for k in range(1, len(options)):
            value = jnp.where(t == k, options[k], value)
        return value

    def logits_pair(q, p):
        pair = pl.ds(pl.multiple_of(p * 2 * rows, 2 * rows), 2 * rows)
        s_ref[block(q), pair] = logit_scale * lax.dot_general(
            im[block(q), :], tx[pair, :], (((1,), (1,)), ((), ())), preferred_element_type=F32
        )

    @pl.when(between)
    def _():
        for h in range(2):
            via_in[h].wait_recv()
            via_out[2 * h].start()
            via_out[2 * h + 1].start()

    copies[IMG_R0].wait_recv()
    same(FWD_R, im, part(zl, 0), right)

    copies[IMG_L1].wait_recv()
    same(FWD_L, im, part(zr, 1), left)
    for h, k in enumerate((TXT_X0, TXT_X1)):
        copies[k].wait_recv()

        @pl.when(jnp.logical_not(turn))
        def _():
            fwd[h].start()

    n_chunks = rows // CHUNK
    n_lane = tile // LANES
    lanes = lambda k: pl.ds(k * LANES, LANES)

    def stats_pair(q, p, order):
        first = p * 2 * rows

        def lane(k):
            return pl.ds(pl.multiple_of(first + k * LANES, LANES), LANES)

        @pl.loop(0, n_chunks, unroll=4)
        def _(r):
            where = pl.ds(pl.multiple_of(q * rows + r * CHUNK, CHUNK), CHUNK)
            parts = [s_ref[where, lane(k)] for k in range(n_lane // 2)]
            top = functools.reduce(jnp.maximum, parts)
            rowp[p, where, :] = top
            rows_s[p, where, :] = functools.reduce(jnp.add, [jnp.exp(v - top) for v in parts])

        @pl.loop(0, n_lane // 2)
        def _(k):
            span = lane(k)
            parts = [s_ref[pl.ds(pl.multiple_of(q * rows + 8 * r, 8), 8), span] for r in range(rows // 8)]
            top = functools.reduce(jnp.maximum, parts)
            at = pl.ds(pl.multiple_of(order * 8, 8), 8)
            colm[at, span] = top
            cols[at, span] = functools.reduce(jnp.add, [jnp.exp(v - top) for v in parts])

    def row_stats(q):
        top = jnp.maximum(rowp[0, block(q), :], rowp[1, block(q), :])
        total = functools.reduce(
            jnp.add, [rows_s[p, block(q), :] * jnp.exp(rowp[p, block(q), :] - top) for p in range(2)]
        )
        top = jnp.transpose(top)
        best = jnp.max(top, axis=0, keepdims=True)
        total = jnp.sum(jnp.transpose(total) * jnp.exp(top - best), axis=0, keepdims=True)
        rstat[:, block(q)] = jnp.broadcast_to(best + jnp.log(total), (8, rows))

    copies[IMG_R1].wait_recv()
    copies[IMG_L0].wait_recv()

    @pl.loop(0, 3)
    def _(t):
        logits_pair(pick(t, z, zl, zr), 0)
        stats_pair(pick(t, z, zl, zr), 0, t)

    for k in (TXT_N0, TXT_N1, FWD_N0, FWD_N1):
        copies[k].wait_recv()

    @pl.loop(0, 3)
    def _(t):
        logits_pair(pick(t, z, zl, zr), 1)
        stats_pair(pick(t, z, zl, zr), 1, t)
        row_stats(pick(t, z, zl, zr))

    copies[FWD_R].wait_recv()
    copies[FWD_L].wait_recv()

    @pl.loop(0, 2)
    def _(p):
        logits_pair(zf, p)
        stats_pair(zf, p, 3)

    row_stats(zf)

    def join(a, c):
        top = jnp.maximum(a, c)
        return top + jnp.log(jnp.exp(a - top) + jnp.exp(c - top))

    rstat[:, block(z)] = join(rstat[:, block(z)], jnp.broadcast_to(rr_ref[...].reshape(1, rows), (8, rows)))
    rl[z] = rstat[...]
    for k, target in ((ROW_R, right), (ROW_L, left), (ROW_F, far)):
        send(k, rstat, rl.at[z], target)
    top = jnp.max(colm[...], axis=0, keepdims=True)
    total = jnp.sum(cols[...] * jnp.exp(colm[...] - top), axis=0, keepdims=True)
    both = jnp.broadcast_to(top + jnp.log(total), (8, tile))
    co[i] = both[:, : 2 * rows]
    cp[2 + i] = both[:, 2 * rows :]
    co[i, :, block(i)] = join(co[i, :, block(i)], jnp.broadcast_to(rc_ref[...].reshape(1, rows), (8, rows)))
    send(OWN_X, co.at[i], co.at[i], across)
    send(OWN_NS, co.at[i], cp.at[i], n_same)
    send(OWN_NO, co.at[i], cp.at[i], n_other)
    send(PRV_X, cp.at[2 + i], cp.at[2 + i], across)
    send(PRV_PS, cp.at[2 + i], co.at[2 + i], p_same)
    send(PRV_PO, cp.at[2 + i], co.at[2 + i], p_other)

    def diag_pass(r, total):
        s = s_ref[pl.ds(pl.multiple_of(z * rows + r * CHUNK, CHUNK), CHUNK), block(i)]
        row = lax.broadcasted_iota(jnp.int32, s.shape, 0) + r * CHUNK
        return total + jnp.where(lax.broadcasted_iota(jnp.int32, s.shape, 1) == row, s, 0.0)

    diag = jnp.sum(lax.fori_loop(0, n_chunks, diag_pass, jnp.zeros((CHUNK, rows), F32)), keepdims=True)

    def merged(parts):
        top = functools.reduce(jnp.maximum, parts)
        return top + jnp.log(functools.reduce(jnp.add, [jnp.exp(p - top) for p in parts]))

    for k in range(ROW_R, PRV_PO + 1):
        copies[k].wait_recv()
    cl[:, : 2 * rows] = merged([co[k] for k in range(4)])
    cl[:, 2 * rows :] = merged([cp[k] for k in range(4)])
    rstat2 = merged([rl[k] for k in range(4)])
    for q in range(4):
        column = jnp.broadcast_to(rstat2[0:1, q * rows : (q + 1) * rows], (LANES, rows))
        rowp[0, pl.ds(q * rows, rows), :] = jnp.transpose(column)

    terms = (
        jnp.sum(rowp[0, block(z), 0:1], keepdims=True)
        + jnp.sum(cl[0:1, block(i)], keepdims=True)
        - 2.0 * diag
    )
    lacc[...] = jnp.broadcast_to(terms, lacc.shape)
    stages = [(z, [right, left, far]), (i, [across])]
    for step, count in blk_stages:
        stages.append(((b // step) % count, [dev(flips(b, step, k), i, z) for k in range(1, count)]))
    first_message = [SUM + sum(len(t) for _, t in stages[:k]) for k in range(len(stages))]

    def loss_send(k):
        place, targets = stages[k]
        terms_ref[k, place] = lacc[...]
        lsnd[k] = lacc[...]
        for j, target in enumerate(targets):
            send(first_message[k] + j, lsnd.at[k], terms_ref.at[k, place], target)

    def loss_next(k):
        targets = stages[k][1]
        for j in range(len(targets)):
            copies[first_message[k] + j].wait_recv()
        lacc[...] = functools.reduce(jnp.add, [terms_ref[k, j] for j in range(len(targets) + 1)])

    def weights_block(q):
        mine = q == z

        @pl.loop(0, n_chunks)
        def _(r):
            where = pl.ds(pl.multiple_of(q * rows + r * CHUNK, CHUNK), CHUNK)
            row_lse = rowp[0, where, :]
            row = lax.broadcasted_iota(jnp.int32, (CHUNK, LANES), 0) + (r * CHUNK + i * rows)
            target = jnp.where(mine, row, -1) - lax.broadcasted_iota(jnp.int32, (CHUNK, LANES), 1)
            for k in range(n_lane):
                s = s_ref[where, lanes(k)]
                value = jnp.exp(s - row_lse) + jnp.exp(s - cl[0:1, lanes(k)])
                if k < n_lane // 2:
                    value = value - jnp.where(target == k * LANES, 2.0, 0.0)
                w[where, lanes(k)] = value.astype(BF16)

    def image_product(q, h):
        return logit_scale * jnp.dot(w[part(q, h), :], tx[...], preferred_element_type=F32)

    def text_product(t):
        return logit_scale * lax.dot_general(
            w[:, block(t)], im[...], (((0,), (0,)), ((), ())), preferred_element_type=F32
        )

    def encode(value, unit, span):
        top = jnp.maximum(jnp.max(jnp.abs(value), axis=0, keepdims=True), 1e-30)
        snd[unit, pl.ds(half, PAD), span] = jnp.broadcast_to(top, (PAD, WIDE)).astype(BF16)
        top = snd[unit, pl.ds(half, PAD), span].astype(F32)[0:1]
        u = value * (POWER_RANGE / top)
        u2 = u * u
        u4 = u2 * u2
        snd[unit, pl.ds(0, half), span] = (u4 * u2 * u).astype(BF16)

    def decode(unit, span):
        code = rcv[unit, pl.ds(0, half), span].astype(F32)
        top = rcv[unit, pl.ds(half, PAD), span].astype(F32)[0:1] * (1.0 / POWER_RANGE)
        size = jnp.abs(code)
        root = jnp.exp2(jnp.log2(size) * (1.0 / 7.0))
        return jnp.where(size > 0.0, jnp.where(code < 0.0, -root, root), 0.0) * top

    def unit_send(unit, target):
        send(OUT + unit, snd.at[unit], rcv.at[unit], target)

    def arrived(unit):
        copies[OUT + unit].wait_recv()

    def columns(body):
        @pl.loop(0, width // WIDE)
        def _(n):
            body(pl.ds(pl.multiple_of(n * WIDE, WIDE), WIDE))

    lo, hi = pl.ds(0, half), pl.ds(half, half)

    def encode_all(ref, where, unit):
        @columns
        def _(span):
            encode(ref[where, span], unit, span)

    loss_send(0)
    weights_block(zf)
    loss_next(0)
    loss_send(1)

    @pl.loop(0, 2)
    def _(u):
        acc[lo, :] = image_product(zf, u)
        encode_all(acc, lo, u)
        remote(OUT + u, snd.at[u], rcv.at[u], dev(b, i, pick(u, zr, zl))).start()

    loss_next(1)
    loss_send(2)

    @pl.loop(0, 3)
    def _(t):
        weights_block(pick(t, zr, zl, z))

    back_turn = b % 8 == 0
    y_first = dev(prv, jnp.where(back_turn, oi, i), z)

    def relay(got, kept, where, out):
        arrived(got)

        @columns
        def _(span):
            encode(kept[where, span] + decode(got, span), out, span)

    for unit, target in ((Y_0, y_first), (Y_1, y_first), (Y_2, p_same), (Y_3, p_same)):
        copies[OUT + unit] = remote(OUT + unit, snd.at[unit], rcv.at[unit], target)
    for unit in (X_0, X_1):
        copies[OUT + unit] = remote(OUT + unit, snd.at[unit], rcv.at[unit], across)

    def relay_text():
        for got, where, out in ((Y_0, lo, X_0), (Y_1, hi, X_1)):
            relay(got, acc, where, out)
            copies[OUT + out].start()

    @pl.loop(0, 3)
    def _(t):
        slot = jnp.where(back_turn, pick(t, oi, 2 + oi, 2 + i), pick(t, 2 + oi, 2 + i, oi))
        acc[...] = text_product(slot)

        @pl.when(jnp.logical_and(back_turn, t == 0))
        def _():
            relay_text()

        @pl.when(slot >= 2)
        def _():
            turned = t - jnp.where(back_turn, 1, 0)
            target = dev(prv, pick(turned, jnp.where(back_turn, oi, i), i), z)
            for h, where in enumerate((lo, hi)):
                unit = Y_0 + 2 * turned + h
                encode_all(acc, where, unit)
                passed_on = jnp.logical_and(back_turn, turned == 1)

                @pl.when(jnp.logical_not(passed_on))
                def _():
                    remote(OUT + unit, snd.at[unit], rcv.at[unit], target).start()

                @pl.when(passed_on)
                def _():
                    pltpu.make_async_remote_copy(
                        src_ref=snd.at[unit],
                        dst_ref=bk.at[h],
                        send_sem=ss.at[OUT + unit],
                        recv_sem=rs.at[BACK_0 + h],
                        device_id=back_dev,
                        device_id_type=MESH,
                    ).start()

    @pl.when(jnp.logical_not(jnp.logical_or(odd, back_turn)))
    def _():
        relay_text()

    @pl.when(turn)
    def _():
        for where, out in ((lo, X_0), (hi, X_1)):
            encode_all(acc, where, out)
            copies[OUT + out].start()

    @pl.loop(0, 4)
    def _(u):
        value = image_product(pick(u, zr, zl, zr, zl), pick(u, 1, 0, 0, 1))
        keep[pick(u, 2, 2, 0, 1)] = value

        @pl.when(u < 2)
        def _():
            encode_all(keep.at[2], slice(None), R_DIR + u)
            remote(
                OUT + R_DIR + u, snd.at[R_DIR + u], rcv.at[R_DIR + u], dev(b, i, pick(u, zr, zl))
            ).start()

    for unit, target in (
        (F_R, right), (F_L, left), (R_DIR, right), (L_DIR, left)
    ):
        copies[OUT + unit] = remote(OUT + unit, snd.at[unit], rcv.at[unit], target)

    @pl.when(jnp.logical_and(odd, jnp.logical_not(turn)))
    def _():
        relay_text()

    loss_next(2)
    loss_send(3)
    relay(F_R, keep.at[0], lo, R_ACC)
    unit_send(R_ACC, right)
    relay(F_L, keep.at[1], lo, L_ACC)
    unit_send(L_ACC, left)
    back_in = [remote(BACK_0 + h, bk.at[h], bk.at[h], back_dev) for h in range(2)]
    back_out = [
        pltpu.make_async_remote_copy(
            src_ref=bk.at[h],
            dst_ref=rcv.at[Y_2 + h],
            send_sem=ss.at[BACK_0 + h],
            recv_sem=rs.at[OUT + Y_2 + h],
            device_id=back_to,
            device_id_type=MESH,
        )
        for h in range(2)
    ]

    @pl.when(backer)
    def _():
        for h in range(2):
            back_in[h].wait_recv()
            back_out[h].start()


    tg_ref[...] = text_product(i)

    @pl.loop(0, 2)
    def _(h):
        ig_ref[pl.ds(pl.multiple_of(h * half, half), half), :] = image_product(z, h)

    loss_next(3)
    loss_ref[...] = lacc[0:1, 0:1] / (2.0 * (n_blk * 8 * rows))

    def add(got, ref, where):
        arrived(got)

        @columns
        def _(span):
            ref[where, span] = ref[where, span] + decode(got, span)

    @pl.when(turn)
    def _():
        for got, where in ((Y_0, lo), (Y_1, hi)):
            add(got, tg_ref, where)

    add(Y_2, tg_ref, lo)
    add(Y_3, tg_ref, hi)
    add(R_DIR, ig_ref, hi)
    add(L_DIR, ig_ref, lo)
    add(R_ACC, ig_ref, lo)
    add(L_ACC, ig_ref, hi)
    add(X_0, tg_ref, lo)
    add(X_1, tg_ref, hi)

    for k, copy in copies.items():
        if k not in (TXT_N0, TXT_N1, FWD_N0, FWD_N1, VIA_0, VIA_1):
            copy.wait_send()
    for role, sent in (
        (turn, via_in), (between, via_out), (jnp.logical_not(turn), own + fwd), (backer, back_out)
    ):

        @pl.when(role)
        def _():
            for copy in sent:
                copy.wait_send()


def shards(n_blk, images, texts, rest_row, rest_col):
    rows, width = images.shape
    tile = 4 * rows
    n_stage, n_sum = 4, 3 + 1 + 3 + 3
    vmem = pl.BlockSpec(memory_space=pltpu.VMEM)
    hbm = pl.BlockSpec(memory_space=pl.ANY)
    image_grad, text_grad, loss = pl.pallas_call(
        functools.partial(kernel, n_blk),
        out_shape=(
            jax.ShapeDtypeStruct((rows, width), F32),
            jax.ShapeDtypeStruct((rows, width), F32),
            jax.ShapeDtypeStruct((1, 1), F32),
        ),
        in_specs=[hbm, hbm, vmem, vmem],
        out_specs=(vmem, vmem, vmem),
        scratch_shapes=[
            pltpu.VMEM((tile, width), BF16),
            pltpu.VMEM((tile, width), BF16),
            pltpu.VMEM((tile, tile), F32),
            pltpu.VMEM((tile, tile), BF16),
            pltpu.VMEM((2, tile, LANES), F32),
            pltpu.VMEM((2, tile, LANES), F32),
            pltpu.VMEM((32, tile), F32),
            pltpu.VMEM((32, tile), F32),
            pltpu.VMEM((8, tile), F32),
            pltpu.VMEM((4, 8, tile), F32),
            pltpu.VMEM((4, 8, 2 * rows), F32),
            pltpu.VMEM((4, 8, 2 * rows), F32),
            pltpu.VMEM((8, tile), F32),
            pltpu.VMEM((3, rows // 2, width), F32),
            pltpu.VMEM((rows, width), F32),
            pltpu.VMEM((rows, width), BF16),
            pltpu.VMEM((2, rows // 2 + PAD, width), BF16),
            pltpu.VMEM((UNITS, rows // 2 + PAD, width), BF16),
            pltpu.VMEM((UNITS, rows // 2 + PAD, width), BF16),
            pltpu.VMEM((8, LANES), F32),
            pltpu.VMEM((n_stage, 8, LANES), F32),
            pltpu.VMEM((n_stage, 4, 8, LANES), F32),
            pltpu.SemaphoreType.DMA((SUM + n_sum,)),
            pltpu.SemaphoreType.DMA((SUM + n_sum,)),
            pltpu.SemaphoreType.DMA((2,)),
        ],
        compiler_params=pltpu.CompilerParams(
            collective_id=0, has_side_effects=True, vmem_limit_bytes=60 << 20
        ),
        cost_estimate=pl.CostEstimate(
            flops=6 * tile * tile * width, bytes_accessed=8 * rows * width * 4, transcendentals=4 * tile * tile
        ),
    )(images, texts, rest_row, rest_col)
    return image_grad, text_grad, loss.reshape(())


def solution(mesh):
    return jax.shard_map(
        functools.partial(shards, mesh.shape["blk"]),
        mesh=mesh,
        in_specs=(
            P(("blk", "node"), None),
            P(("blk", "node"), None),
            P(("blk", "node")),
            P(("blk", "node")),
        ),
        out_specs=(P(("blk", "node"), None), P(("blk", "node"), None), P()),
        check_vma=False,
    )
```

```python
import functools

import jax
import jax.numpy as jnp
from jax import lax
from jax.experimental import pallas as pl
from jax.experimental.pallas import tpu as pltpu
from jax.sharding import PartitionSpec as P


MESH = pl.DeviceIdType.MESH
F32, BF16 = jnp.float32, jnp.bfloat16
logit_scale = 100.0
LANES = 128
CHUNK = 16
PAD = 16
WIDE = 256
POWER_RANGE = 2.0**18

(IMG_R0, IMG_R1, IMG_L1, IMG_L0, FWD_R, FWD_L, TXT_X0, TXT_X1, TXT_N0, TXT_N1, FWD_N0, FWD_N1) = range(12)
(ROW_R, ROW_L, ROW_F, OWN_X, OWN_NS, OWN_NO, PRV_X, PRV_PS, PRV_PO) = range(12, 21)
(VIA_0, VIA_1, VIA_S0, VIA_S1, VIA_O0, VIA_O1) = range(21, 27)
(BACK_0, BACK_1) = range(27, 29)
OUT = 29
(F_R, F_L, R_DIR, L_DIR, R_ACC, L_ACC, Y_0, Y_1, Y_2, Y_3, X_0, X_1) = range(12)
UNITS = 12
SUM = OUT + UNITS


def kernel(
    n_blk, img_ref, txt_ref, rr_ref, rc_ref, ig_ref, tg_ref, loss_ref,
    im, tx, s_ref, w, rowp, rows_s, colm, cols, rstat, rl, co, cp, cl, keep, acc, via, bk, snd, rcv, lacc, lsnd, terms_ref,
    ss, rs, lsem,
):
    rows, width = img_ref.shape
    half = rows // 2
    tile = 4 * rows
    b = lax.axis_index("blk")
    node = lax.axis_index("node")
    i, z = node // 4, node % 4
    zr, zl, zf = (z + 1) % 4, (z + 3) % 4, (z + 2) % 4
    nxt, prv = (b + 1) % n_blk, (b + n_blk - 1) % n_blk
    oi = 1 - i

    def dev(blk, hi, zz):
        return (blk, hi * 4 + zz)

    right, left, far = dev(b, i, zr), dev(b, i, zl), dev(b, i, zf)
    across = dev(b, oi, z)
    n_same, n_other, p_same, p_other = dev(nxt, i, z), dev(nxt, oi, z), dev(prv, i, z), dev(prv, oi, z)

    def flip(value, step):
        return value + step - 2 * step * ((value // step) % 2)

    def flips(value, step, k):
        if k % 2:
            value = flip(value, step)
        return flip(value, 2 * step) if k // 2 else value

    blk_stages, step = [], 1
    while step < n_blk:
        count = min(4, n_blk // step)
        blk_stages.append((step, count))
        step *= count

    load_img = pltpu.make_async_copy(img_ref, im.at[pl.ds(pl.multiple_of(z * rows, rows), rows)], lsem.at[0])
    load_txt = pltpu.make_async_copy(txt_ref, tx.at[pl.ds(pl.multiple_of(i * rows, rows), rows)], lsem.at[1])
    load_img.start()
    load_txt.start()

    barrier = pltpu.get_barrier_semaphore()
    partners = [right, left, far, across, n_same, n_other, p_same, p_other]
    for step, count in blk_stages:
        partners += [dev(flips(b, step, k), i, z) for k in range(1, count) if step * k != 1]
    for partner in partners:
        pl.semaphore_signal(barrier, inc=1, device_id=partner, device_id_type=MESH)

    turn, between, ahead = b % 8 == 7, b % 8 == 1, b % 8 == 0
    via_dev = dev((b + n_blk - 6) % n_blk, i, z)
    via_from = dev((b + 6) % n_blk, i, z)
    via_same, via_other = dev((b + 7) % n_blk, i, z), dev((b + 7) % n_blk, oi, z)
    from_same, from_other = dev((b + n_blk - 7) % n_blk, i, z), dev((b + n_blk - 7) % n_blk, oi, z)
    backer = b % 8 == 6
    back_dev, back_src = dev((b + 6) % n_blk, i, z), dev((b + 7) % n_blk, i, z)
    back_from, back_to = dev((b + n_blk - 6) % n_blk, i, z), dev((b + n_blk - 7) % n_blk, i, z)
    for role, others in (
        (turn, [via_dev, back_src]),
        (between, [via_from, via_same, via_other]),
        (ahead, [from_same, from_other, back_dev]),
        (backer, [back_from, back_to]),
    ):

        @pl.when(role)
        def _():
            for partner in others:
                pl.semaphore_signal(barrier, inc=1, device_id=partner, device_id_type=MESH)

    extra = jnp.where(turn, 2, 0) + jnp.where(between, 3, 0) + jnp.where(ahead, 3, 0) + jnp.where(backer, 2, 0)
    pl.semaphore_wait(barrier, len(partners) + extra)
    load_img.wait()
    load_txt.wait()

    def remote(k, src, dst, target):
        return pltpu.make_async_remote_copy(
            src_ref=src, dst_ref=dst, send_sem=ss.at[k], recv_sem=rs.at[k], device_id=target, device_id_type=MESH
        )

    def block(slot):
        return pl.ds(pl.multiple_of(slot * rows, rows), rows)

    def part(slot, h):
        return pl.ds(pl.multiple_of(slot * rows + h * half, half), half)

    copies = {}

    def send(k, src, dst, target):
        copies[k] = remote(k, src, dst, target)
        copies[k].start()

    def same(k, ref, where, target):
        send(k, ref.at[where], ref.at[where], target)

    odd = b % 2 == 1

    def start(k, src, dst, target):
        copies[k] = remote(k, src, dst, target)
        return copies[k]

    same(IMG_R0, im, part(z, 0), right)
    same(IMG_L1, im, part(z, 1), left)
    own = [
        start(k, tx.at[part(i, h)], tx.at[part(2 + i, h)], n_same) for h, k in enumerate((TXT_N0, TXT_N1))
    ]

    via_in = [start(k, tx.at[part(i, h)], via.at[pl.ds(h * half, half)], via_dev) for h, k in enumerate((VIA_0, VIA_1))]
    via_out = [
        pltpu.make_async_remote_copy(
            src_ref=via.at[pl.ds(h * half, half)],
            dst_ref=tx.at[part(2 + i, h)],
            send_sem=ss.at[k],
            recv_sem=rs.at[landing],
            device_id=target,
            device_id_type=MESH,
        )
        for h, k, landing, target in (
            (0, VIA_S0, TXT_N0, via_same), (0, VIA_O0, FWD_N0, via_other),
            (1, VIA_S1, TXT_N1, via_same), (1, VIA_O1, FWD_N1, via_other),
        )
    ]

    @pl.when(turn)
    def _():
        via_in[0].start()
        via_in[1].start()

    @pl.when(jnp.logical_not(turn))
    def _():
        own[0].start()
        own[1].start()

    swap = [start(k, tx.at[part(i, h)], tx.at[part(i, h)], across) for h, k in enumerate((TXT_X0, TXT_X1))]

    swap[0].start()
    swap[1].start()

    same(IMG_R1, im, part(z, 1), right)
    same(IMG_L0, im, part(z, 0), left)
    fwd = [
        start(k, tx.at[part(oi, h)], tx.at[part(2 + oi, h)], n_same) for h, k in enumerate((FWD_N0, FWD_N1))
    ]

    def pick(t, *options):
        value = options[0]
        for k in range(1, len(options)):
            value = jnp.where(t == k, options[k], value)
        return value

    def logits_pair(q, p):
        pair = pl.ds(pl.multiple_of(p * 2 * rows, 2 * rows), 2 * rows)
        s_ref[block(q), pair] = logit_scale * lax.dot_general(
            im[block(q), :], tx[pair, :], (((1,), (1,)), ((), ())), preferred_element_type=F32
        )

    @pl.when(between)
    def _():
        for h in range(2):
            via_in[h].wait_recv()
            via_out[2 * h].start()
            via_out[2 * h + 1].start()

    copies[IMG_R0].wait_recv()
    same(FWD_R, im, part(zl, 0), right)

    copies[IMG_L1].wait_recv()
    same(FWD_L, im, part(zr, 1), left)
    for h, k in enumerate((TXT_X0, TXT_X1)):
        copies[k].wait_recv()

        @pl.when(jnp.logical_not(turn))
        def _():
            fwd[h].start()

    n_chunks = rows // CHUNK
    n_lane = tile // LANES
    lanes = lambda k: pl.ds(k * LANES, LANES)

    def stats_pair(q, p, order):
        first = p * 2 * rows

        def lane(k):
            return pl.ds(pl.multiple_of(first + k * LANES, LANES), LANES)

        @pl.loop(0, n_chunks, unroll=4)
        def _(r):
            where = pl.ds(pl.multiple_of(q * rows + r * CHUNK, CHUNK), CHUNK)
            parts = [s_ref[where, lane(k)] for k in range(n_lane // 2)]
            top = functools.reduce(jnp.maximum, parts)
            rowp[p, where, :] = top
            rows_s[p, where, :] = functools.reduce(jnp.add, [jnp.exp(v - top) for v in parts])

        @pl.loop(0, n_lane // 2)
        def _(k):
            span = lane(k)
            parts = [s_ref[pl.ds(pl.multiple_of(q * rows + 8 * r, 8), 8), span] for r in range(rows // 8)]
            top = functools.reduce(jnp.maximum, parts)
            at = pl.ds(pl.multiple_of(order * 8, 8), 8)
            colm[at, span] = top
            cols[at, span] = functools.reduce(jnp.add, [jnp.exp(v - top) for v in parts])

    def row_stats(q):
        top = jnp.maximum(rowp[0, block(q), :], rowp[1, block(q), :])
        total = functools.reduce(
            jnp.add, [rows_s[p, block(q), :] * jnp.exp(rowp[p, block(q), :] - top) for p in range(2)]
        )
        top = jnp.transpose(top)
        best = jnp.max(top, axis=0, keepdims=True)
        total = jnp.sum(jnp.transpose(total) * jnp.exp(top - best), axis=0, keepdims=True)
        rstat[:, block(q)] = jnp.broadcast_to(best + jnp.log(total), (8, rows))

    copies[IMG_R1].wait_recv()
    copies[IMG_L0].wait_recv()

    @pl.loop(0, 3)
    def _(t):
        logits_pair(pick(t, z, zl, zr), 0)
        stats_pair(pick(t, z, zl, zr), 0, t)

    for k in (TXT_N0, TXT_N1, FWD_N0, FWD_N1):
        copies[k].wait_recv()

    @pl.loop(0, 3)
    def _(t):
        logits_pair(pick(t, z, zl, zr), 1)
        stats_pair(pick(t, z, zl, zr), 1, t)
        row_stats(pick(t, z, zl, zr))

    copies[FWD_R].wait_recv()
    copies[FWD_L].wait_recv()

    @pl.loop(0, 2)
    def _(p):
        logits_pair(zf, p)
        stats_pair(zf, p, 3)

    row_stats(zf)

    def join(a, c):
        top = jnp.maximum(a, c)
        return top + jnp.log(jnp.exp(a - top) + jnp.exp(c - top))

    rstat[:, block(z)] = join(rstat[:, block(z)], jnp.broadcast_to(rr_ref[...].reshape(1, rows), (8, rows)))
    rl[z] = rstat[...]
    for k, target in ((ROW_R, right), (ROW_L, left), (ROW_F, far)):
        send(k, rstat, rl.at[z], target)
    top = jnp.max(colm[...], axis=0, keepdims=True)
    total = jnp.sum(cols[...] * jnp.exp(colm[...] - top), axis=0, keepdims=True)
    both = jnp.broadcast_to(top + jnp.log(total), (8, tile))
    co[i] = both[:, : 2 * rows]
    cp[2 + i] = both[:, 2 * rows :]
    co[i, :, block(i)] = join(co[i, :, block(i)], jnp.broadcast_to(rc_ref[...].reshape(1, rows), (8, rows)))
    send(OWN_X, co.at[i], co.at[i], across)
    send(OWN_NS, co.at[i], cp.at[i], n_same)
    send(OWN_NO, co.at[i], cp.at[i], n_other)
    send(PRV_X, cp.at[2 + i], cp.at[2 + i], across)
    send(PRV_PS, cp.at[2 + i], co.at[2 + i], p_same)
    send(PRV_PO, cp.at[2 + i], co.at[2 + i], p_other)

    def diag_pass(r, total):
        s = s_ref[pl.ds(pl.multiple_of(z * rows + r * CHUNK, CHUNK), CHUNK), block(i)]
        row = lax.broadcasted_iota(jnp.int32, s.shape, 0) + r * CHUNK
        return total + jnp.where(lax.broadcasted_iota(jnp.int32, s.shape, 1) == row, s, 0.0)

    diag = jnp.sum(lax.fori_loop(0, n_chunks, diag_pass, jnp.zeros((CHUNK, rows), F32)), keepdims=True)

    def merged(parts):
        top = functools.reduce(jnp.maximum, parts)
        return top + jnp.log(functools.reduce(jnp.add, [jnp.exp(p - top) for p in parts]))

    for k in range(ROW_R, PRV_PO + 1):
        copies[k].wait_recv()
    cl[:, : 2 * rows] = merged([co[k] for k in range(4)])
    cl[:, 2 * rows :] = merged([cp[k] for k in range(4)])
    rstat2 = merged([rl[k] for k in range(4)])
    for q in range(4):
        column = jnp.broadcast_to(rstat2[0:1, q * rows : (q + 1) * rows], (LANES, rows))
        rowp[0, pl.ds(q * rows, rows), :] = jnp.transpose(column)

    terms = (
        jnp.sum(rowp[0, block(z), 0:1], keepdims=True)
        + jnp.sum(cl[0:1, block(i)], keepdims=True)
        - 2.0 * diag
    )
    lacc[...] = jnp.broadcast_to(terms, lacc.shape)
    stages = [(z, [right, left, far]), (i, [across])]
    for step, count in blk_stages:
        stages.append(((b // step) % count, [dev(flips(b, step, k), i, z) for k in range(1, count)]))
    first_message = [SUM + sum(len(t) for _, t in stages[:k]) for k in range(len(stages))]

    def loss_send(k):
        place, targets = stages[k]
        terms_ref[k, place] = lacc[...]
        lsnd[k] = lacc[...]
        for j, target in enumerate(targets):
            send(first_message[k] + j, lsnd.at[k], terms_ref.at[k, place], target)

    def loss_next(k):
        targets = stages[k][1]
        for j in range(len(targets)):
            copies[first_message[k] + j].wait_recv()
        lacc[...] = functools.reduce(jnp.add, [terms_ref[k, j] for j in range(len(targets) + 1)])

    def weights_block(q):
        mine = q == z

        @pl.loop(0, n_chunks)
        def _(r):
            where = pl.ds(pl.multiple_of(q * rows + r * CHUNK, CHUNK), CHUNK)
            row_lse = rowp[0, where, :]
            row = lax.broadcasted_iota(jnp.int32, (CHUNK, LANES), 0) + (r * CHUNK + i * rows)
            target = jnp.where(mine, row, -1) - lax.broadcasted_iota(jnp.int32, (CHUNK, LANES), 1)
            for k in range(n_lane):
                s = s_ref[where, lanes(k)]
                value = jnp.exp(s - row_lse) + jnp.exp(s - cl[0:1, lanes(k)])
                if k < n_lane // 2:
                    value = value - jnp.where(target == k * LANES, 2.0, 0.0)
                w[where, lanes(k)] = value.astype(BF16)

    def image_product(q, h):
        return logit_scale * jnp.dot(w[part(q, h), :], tx[...], preferred_element_type=F32)

    def text_product(t):
        return logit_scale * lax.dot_general(
            w[:, block(t)], im[...], (((0,), (0,)), ((), ())), preferred_element_type=F32
        )

    def encode(value, unit, span):
        top = jnp.maximum(jnp.max(jnp.abs(value), axis=0, keepdims=True), 1e-30)
        snd[unit, pl.ds(half, PAD), span] = jnp.broadcast_to(top, (PAD, WIDE)).astype(BF16)
        top = snd[unit, pl.ds(half, PAD), span].astype(F32)[0:1]
        u = value * (POWER_RANGE / top)
        u2 = u * u
        u4 = u2 * u2
        snd[unit, pl.ds(0, half), span] = (u4 * u2 * u).astype(BF16)

    def decode(unit, span):
        code = rcv[unit, pl.ds(0, half), span].astype(F32)
        top = rcv[unit, pl.ds(half, PAD), span].astype(F32)[0:1] * (1.0 / POWER_RANGE)
        size = jnp.abs(code)
        root = jnp.exp2(jnp.log2(size) * (1.0 / 7.0))
        return jnp.where(size > 0.0, jnp.where(code < 0.0, -root, root), 0.0) * top

    def unit_send(unit, target):
        send(OUT + unit, snd.at[unit], rcv.at[unit], target)

    def arrived(unit):
        copies[OUT + unit].wait_recv()

    def columns(body):
        @pl.loop(0, width // WIDE)
        def _(n):
            body(pl.ds(pl.multiple_of(n * WIDE, WIDE), WIDE))

    lo, hi = pl.ds(0, half), pl.ds(half, half)

    def encode_all(ref, where, unit):
        @columns
        def _(span):
            encode(ref[where, span], unit, span)

    loss_send(0)
    weights_block(zf)
    loss_next(0)
    loss_send(1)

    @pl.loop(0, 2)
    def _(u):
        acc[lo, :] = image_product(zf, u)
        encode_all(acc, lo, u)
        remote(OUT + u, snd.at[u], rcv.at[u], dev(b, i, pick(u, zr, zl))).start()

    loss_next(1)
    loss_send(2)

    @pl.loop(0, 3)
    def _(t):
        weights_block(pick(t, zr, zl, z))

    back_turn = b % 8 == 0
    y_first = dev(prv, jnp.where(back_turn, oi, i), z)

    def relay(got, kept, where, out):
        arrived(got)

        @columns
        def _(span):
            encode(kept[where, span] + decode(got, span), out, span)

    for unit, target in ((Y_0, y_first), (Y_1, y_first), (Y_2, p_same), (Y_3, p_same)):
        copies[OUT + unit] = remote(OUT + unit, snd.at[unit], rcv.at[unit], target)
    for unit in (X_0, X_1):
        copies[OUT + unit] = remote(OUT + unit, snd.at[unit], rcv.at[unit], across)

    def relay_text():
        for got, where, out in ((Y_0, lo, X_0), (Y_1, hi, X_1)):
            relay(got, acc, where, out)
            copies[OUT + out].start()

    @pl.loop(0, 3)
    def _(t):
        slot = jnp.where(back_turn, pick(t, oi, 2 + oi, 2 + i), pick(t, 2 + oi, 2 + i, oi))
        acc[...] = text_product(slot)

        @pl.when(jnp.logical_and(back_turn, t == 0))
        def _():
            relay_text()

        @pl.when(slot >= 2)
        def _():
            turned = t - jnp.where(back_turn, 1, 0)
            target = dev(prv, pick(turned, jnp.where(back_turn, oi, i), i), z)
            for h, where in enumerate((lo, hi)):
                unit = Y_0 + 2 * turned + h
                encode_all(acc, where, unit)
                passed_on = jnp.logical_and(back_turn, turned == 1)

                @pl.when(jnp.logical_not(passed_on))
                def _():
                    remote(OUT + unit, snd.at[unit], rcv.at[unit], target).start()

                @pl.when(passed_on)
                def _():
                    pltpu.make_async_remote_copy(
                        src_ref=snd.at[unit],
                        dst_ref=bk.at[h],
                        send_sem=ss.at[OUT + unit],
                        recv_sem=rs.at[BACK_0 + h],
                        device_id=back_dev,
                        device_id_type=MESH,
                    ).start()

    @pl.when(jnp.logical_not(jnp.logical_or(odd, back_turn)))
    def _():
        relay_text()

    @pl.when(turn)
    def _():
        for where, out in ((lo, X_0), (hi, X_1)):
            encode_all(acc, where, out)
            copies[OUT + out].start()

    @pl.loop(0, 4)
    def _(u):
        value = image_product(pick(u, zr, zl, zr, zl), pick(u, 1, 0, 0, 1))
        keep[pick(u, 2, 2, 0, 1)] = value

        @pl.when(u < 2)
        def _():
            encode_all(keep.at[2], slice(None), R_DIR + u)
            remote(
                OUT + R_DIR + u, snd.at[R_DIR + u], rcv.at[R_DIR + u], dev(b, i, pick(u, zr, zl))
            ).start()

    for unit, target in (
        (F_R, right), (F_L, left), (R_DIR, right), (L_DIR, left)
    ):
        copies[OUT + unit] = remote(OUT + unit, snd.at[unit], rcv.at[unit], target)

    @pl.when(jnp.logical_and(odd, jnp.logical_not(turn)))
    def _():
        relay_text()

    loss_next(2)
    loss_send(3)
    relay(F_R, keep.at[0], lo, R_ACC)
    unit_send(R_ACC, right)
    relay(F_L, keep.at[1], lo, L_ACC)
    unit_send(L_ACC, left)
    back_in = [remote(BACK_0 + h, bk.at[h], bk.at[h], back_dev) for h in range(2)]
    back_out = [
        pltpu.make_async_remote_copy(
            src_ref=bk.at[h],
            dst_ref=rcv.at[Y_2 + h],
            send_sem=ss.at[BACK_0 + h],
            recv_sem=rs.at[OUT + Y_2 + h],
            device_id=back_to,
            device_id_type=MESH,
        )
        for h in range(2)
    ]

    @pl.when(backer)
    def _():
        for h in range(2):
            back_in[h].wait_recv()
            back_out[h].start()


    tg_ref[...] = text_product(i)

    @pl.loop(0, 2)
    def _(h):
        ig_ref[pl.ds(pl.multiple_of(h * half, half), half), :] = image_product(z, h)


    def add(got, ref, where):
        arrived(got)

        @columns
        def _(span):
            ref[where, span] = ref[where, span] + decode(got, span)

    def add_back():
        add(Y_2, tg_ref, lo)
        add(Y_3, tg_ref, hi)

    @pl.when(jnp.logical_not(turn))
    def _():
        add_back()

    add(R_DIR, ig_ref, hi)
    add(L_DIR, ig_ref, lo)
    add(R_ACC, ig_ref, lo)
    add(L_ACC, ig_ref, hi)
    add(X_0, tg_ref, lo)
    add(X_1, tg_ref, hi)

    @pl.when(turn)
    def _():
        add_back()
        for got, where in ((Y_0, lo), (Y_1, hi)):
            add(got, tg_ref, where)

    loss_next(3)
    loss_ref[...] = lacc[0:1, 0:1] / (2.0 * (n_blk * 8 * rows))
    for k, copy in copies.items():
        if k not in (TXT_N0, TXT_N1, FWD_N0, FWD_N1, VIA_0, VIA_1):
            copy.wait_send()
    for role, sent in (
        (turn, via_in), (between, via_out), (jnp.logical_not(turn), own + fwd), (backer, back_out)
    ):

        @pl.when(role)
        def _():
            for copy in sent:
                copy.wait_send()


def shards(n_blk, images, texts, rest_row, rest_col):
    rows, width = images.shape
    tile = 4 * rows
    n_stage, n_sum = 4, 3 + 1 + 3 + 3
    vmem = pl.BlockSpec(memory_space=pltpu.VMEM)
    hbm = pl.BlockSpec(memory_space=pl.ANY)
    image_grad, text_grad, loss = pl.pallas_call(
        functools.partial(kernel, n_blk),
        out_shape=(
            jax.ShapeDtypeStruct((rows, width), F32),
            jax.ShapeDtypeStruct((rows, width), F32),
            jax.ShapeDtypeStruct((1, 1), F32),
        ),
        in_specs=[hbm, hbm, vmem, vmem],
        out_specs=(vmem, vmem, vmem),
        scratch_shapes=[
            pltpu.VMEM((tile, width), BF16),
            pltpu.VMEM((tile, width), BF16),
            pltpu.VMEM((tile, tile), F32),
            pltpu.VMEM((tile, tile), BF16),
            pltpu.VMEM((2, tile, LANES), F32),
            pltpu.VMEM((2, tile, LANES), F32),
            pltpu.VMEM((32, tile), F32),
            pltpu.VMEM((32, tile), F32),
            pltpu.VMEM((8, tile), F32),
            pltpu.VMEM((4, 8, tile), F32),
            pltpu.VMEM((4, 8, 2 * rows), F32),
            pltpu.VMEM((4, 8, 2 * rows), F32),
            pltpu.VMEM((8, tile), F32),
            pltpu.VMEM((3, rows // 2, width), F32),
            pltpu.VMEM((rows, width), F32),
            pltpu.VMEM((rows, width), BF16),
            pltpu.VMEM((2, rows // 2 + PAD, width), BF16),
            pltpu.VMEM((UNITS, rows // 2 + PAD, width), BF16),
            pltpu.VMEM((UNITS, rows // 2 + PAD, width), BF16),
            pltpu.VMEM((8, LANES), F32),
            pltpu.VMEM((n_stage, 8, LANES), F32),
            pltpu.VMEM((n_stage, 4, 8, LANES), F32),
            pltpu.SemaphoreType.DMA((SUM + n_sum,)),
            pltpu.SemaphoreType.DMA((SUM + n_sum,)),
            pltpu.SemaphoreType.DMA((2,)),
        ],
        compiler_params=pltpu.CompilerParams(
            collective_id=0, has_side_effects=True, vmem_limit_bytes=60 << 20
        ),
        cost_estimate=pl.CostEstimate(
            flops=6 * tile * tile * width, bytes_accessed=8 * rows * width * 4, transcendentals=4 * tile * tile
        ),
    )(images, texts, rest_row, rest_col)
    return image_grad, text_grad, loss.reshape(())


def solution(mesh):
    return jax.shard_map(
        functools.partial(shards, mesh.shape["blk"]),
        mesh=mesh,
        in_specs=(
            P(("blk", "node"), None),
            P(("blk", "node"), None),
            P(("blk", "node")),
            P(("blk", "node")),
        ),
        out_specs=(P(("blk", "node"), None), P(("blk", "node"), None), P()),
        check_vma=False,
    )
```
